256 devices in a mesh: gz: 32 (over y_lo, z, core), ta: 8 (over y_hi, x).
Axes of the slice: x: 4, y: 4 (y_hi: 2, y_lo: 2; y = y_hi * 2 + y_lo), z: 8, core: 2. Of those that a mesh axis runs over, the one named last changes fastest.
Arguments:
- outputs_fwd: bfloat16 [16, 64, 64, 1280], P('ta', 'gz'), may hold values from -6 to 6
- cotangent: bfloat16 [16, 64, 64, 1280], P('ta', 'gz'), may hold values from -6 to 6
- spatial_weight: bfloat16 [3, 64, 288], replicated, may hold values from -0.21875 to 0.21875
- hidden_bias: float32 [64], replicated, may hold values from -1 to 1
- temporal_weight: bfloat16 [3, 32, 64], replicated, may hold values from -0.4375 to 0.4375
Outputs:
- rebuilt: bfloat16 [16, 64, 32, 1280], P('ta', 'gz')
- grad_in: bfloat16 [16, 64, 32, 1280], P('ta', 'gz')
- grad_spatial: float32 [3, 64, 288], replicated
- grad_bias: float32 [64], replicated
- grad_temporal: float32 [3, 32, 64], replicated
The draws below stay inside these ranges and needn't reach their ends.
All inputs are finite; a program needn't handle non-finite values.
Results may differ from the reference program's by a relative error of at most 0.0075.
Values may be sent and summed in bfloat16 or wider, within the bound.
No kernel may reach another device: no remote copies, remote signals or barrier semaphores. Data moves between devices by JAX's collectives and lax.ppermute only.
A program may use at most 64 MiB of HBM per device.

```python
import math
import jax
import jax.numpy as jnp
from jax import lax

CH = 32
HID = 64
ROWS = 8
COLS = 160
NZ = 64
FRAMES = 16


def level_of(stream_key, dims, split, smallest, high):
    def one(axis_at, parts):
        heights = jax.random.uniform(jax.random.fold_in(jax.random.fold_in(stream_key, 6), axis_at), (parts,), jnp.float32, smallest / len(split), high / len(split))
        return jnp.repeat(jnp.exp(heights), dims[axis_at] // parts).reshape((-1,) + (1,) * (len(dims) - axis_at - 1))

    gain = one(*split[0])
    for cut in split[1:]:
        gain = gain * one(*cut)
    return gain


def bell_draw(stream_key, dims, scale, bound, split=(), kind=jnp.bfloat16):
    drawn = jax.random.normal(stream_key, dims, jnp.float32) * scale
    if len(split) > 0:
        drawn = level_of(stream_key, dims, split, -0.22, 0.18) * drawn
    return jnp.clip(drawn, min=-bound, max=bound).astype(kind)


def setup_inputs(seed: int = 0) -> dict:
    splits = jax.random.split(jax.random.key(seed), 6)
    return {
        "outputs_fwd": bell_draw(splits[0], (FRAMES, NZ, 2 * CH, ROWS * COLS), 1.0, 6.0, ((0, 8), (1, 32))),
        "cotangent": bell_draw(splits[1], (FRAMES, NZ, 2 * CH, ROWS * COLS), 1.0, 6.0, ((0, 8), (1, 32))),
        "spatial_weight": bell_draw(splits[2], (3, HID, 9 * CH), (27 * CH) ** -0.5, 0.21875),
        "hidden_bias": jnp.clip(jax.random.uniform(splits[3], (HID,), jnp.float32, -1.0, 1.0), -1.0, 1.0),
        "temporal_weight": bell_draw(splits[4], (3, CH, HID), (3 * HID) ** -0.5, 0.4375),
    }


def unfold(field):
    leading = field.shape[:-1]
    planar = field.reshape(leading + (ROWS, COLS))
    padded = jnp.pad(planar, [(0, 0)] * len(leading) + [(1, 1), (1, 1)])
    windows = [padded[..., row_off:row_off + ROWS, col_off:col_off + COLS] for row_off in range(3) for col_off in range(3)]
    stacked = jnp.stack(windows, axis=-4)
    return stacked.reshape(leading[:-1] + (9 * leading[-1], ROWS * COLS))

def linear_frame(frame_in, spatial_weight):
    columns = jnp.pad(unfold(frame_in), ((1, 1), (0, 0), (0, 0))).astype(jnp.float32)
    weight = spatial_weight.astype(jnp.float32)
    total = jnp.einsum('oi,zir->zor', weight[0], columns[0:NZ], precision=lax.Precision.HIGHEST)
    total = total + jnp.einsum('oi,zir->zor', weight[1], columns[1:NZ + 1], precision=lax.Precision.HIGHEST)
    total = total + jnp.einsum('oi,zir->zor', weight[2], columns[2:NZ + 2], precision=lax.Precision.HIGHEST)
    return total

def reference(outputs_fwd, cotangent, spatial_weight, hidden_bias, temporal_weight):
    front_half = outputs_fwd[:, :, :CH]
    back_half = outputs_fwd[:, :, CH:]
    grad_front = cotangent[:, :, :CH]
    grad_back = cotangent[:, :, CH:]
    bias_col = hidden_bias.astype(jnp.float32)[None, :, None]

    def activate(frame_in):
        return jax.nn.silu(linear_frame(frame_in, spatial_weight) + bias_col).astype(jnp.bfloat16)
    active = lax.map(activate, front_half)
    tweight = temporal_weight.astype(jnp.float32)

    def frame_step(carry, index):
        spatial_acc, bias_acc, temporal_acc = carry
        near = [active[(index + offset - 1) % FRAMES].astype(jnp.float32) for offset in range(3)]
        mapped = jnp.einsum('oi,zir->zor', tweight[0], near[0], precision=lax.Precision.HIGHEST)
        mapped = mapped + jnp.einsum('oi,zir->zor', tweight[1], near[1], precision=lax.Precision.HIGHEST)
        mapped = mapped + jnp.einsum('oi,zir->zor', tweight[2], near[2], precision=lax.Precision.HIGHEST)
        rebuilt = (back_half[index].astype(jnp.float32) - mapped).astype(jnp.bfloat16)
        grads_near = [grad_back[(index + 1 - offset) % FRAMES].astype(jnp.float32) for offset in range(3)]
        through = jnp.einsum('oi,zor->zir', tweight[0], grads_near[0], precision=lax.Precision.HIGHEST)
        through = through + jnp.einsum('oi,zor->zir', tweight[1], grads_near[1], precision=lax.Precision.HIGHEST)
        through = through + jnp.einsum('oi,zor->zir', tweight[2], grads_near[2], precision=lax.Precision.HIGHEST)
        own_grad = grad_back[index].astype(jnp.float32)
        temporal_acc = temporal_acc + jnp.stack([jnp.einsum('zor,zir->oi', own_grad, near[offset], precision=lax.Precision.HIGHEST) for offset in range(3)])
        frame_in = front_half[index]
        linear_val, pullback = jax.vjp(lambda field: linear_frame(field, spatial_weight), frame_in.astype(jnp.float32))
        hidden_in = linear_val + bias_col
        sigmoid_val = jax.nn.sigmoid(hidden_in)
        hidden_grad = (through * sigmoid_val * (1.0 + hidden_in * (1.0 - sigmoid_val))).astype(jnp.bfloat16)
        grad_value = hidden_grad.astype(jnp.float32)
        columns = jnp.pad(unfold(frame_in), ((1, 1), (0, 0), (0, 0))).astype(jnp.float32)
        spatial_acc = spatial_acc + jnp.stack([jnp.einsum('zor,zir->oi', grad_value, columns[depth:depth + NZ], precision=lax.Precision.HIGHEST) for depth in range(3)])
        bias_acc = bias_acc + lax.optimization_barrier(jnp.sum(grad_value, axis=(0, 2)))
        input_grad = pullback(grad_value)[0]
        grad_in = (grad_front[index].astype(jnp.float32) + input_grad).astype(jnp.bfloat16)
        return ((spatial_acc, bias_acc, temporal_acc), (rebuilt, grad_in))
    start = (jnp.zeros(spatial_weight.shape, jnp.float32), jnp.zeros((HID,), jnp.float32), jnp.zeros(temporal_weight.shape, jnp.float32))
    carry, (rebuilt, grad_in) = lax.scan(frame_step, start, jnp.arange(FRAMES, dtype=jnp.int32))
    factor = 1.0 / math.sqrt(FRAMES * NZ * ROWS * COLS)
    return (rebuilt, grad_in, carry[0] * factor, carry[1] * factor, carry[2] * factor)
```

```python
import math

import jax
import jax.numpy as jnp
from jax import lax
from jax.experimental import pallas as pl
from jax.experimental.pallas import tpu as pltpu
from jax.sharding import PartitionSpec as P

ROWS = 8
COLS = 160
PIX = ROWS * COLS
CH = 32
HID = 64
WIN = 9 * CH
F32 = jnp.float32
BF16 = jnp.bfloat16
VMEM_LIMIT = 48 * 1024 * 1024


def nn(a, b):
    return lax.dot_general(a, b, (((1,), (0,)), ((), ())), preferred_element_type=F32)


def nt(a, b):
    return lax.dot_general(a, b, (((1,), (1,)), ((), ())), preferred_element_type=F32)


def moved_rows(field, rows):
    if rows == 0:
        return field
    edge = jnp.zeros((field.shape[0], COLS), field.dtype)
    if rows > 0:
        return jnp.concatenate([field[:, COLS:], edge], axis=1)
    return jnp.concatenate([edge, field[:, : PIX - COLS]], axis=1)


def moved_cols(field, cols, col_of):
    if cols == 0:
        return field
    rolled = pltpu.roll(field, (-cols) % PIX, 1)
    return jnp.where(col_of == (COLS - 1 if cols > 0 else 0), jnp.zeros_like(rolled), rolled)


def hidden_kernel(
    y1_ref, low_ref, high_ref, g2_ref, before_ref, after_ref, sw_ref, bias_ref, tw_ref,
    active_ref, hgrad_ref, pay_ref,
    columns, cots,
):
    col_of = lax.rem(lax.broadcasted_iota(jnp.int32, (CH, PIX), 1), COLS)
    weight = jnp.concatenate([sw_ref[0], sw_ref[1], sw_ref[2]], axis=1)
    bias = bias_ref[...]
    tback = jnp.concatenate([tw_ref[2], tw_ref[1], tw_ref[0]], axis=0)
    for z in range(2):
        cots[z, 0:32] = before_ref[0, z]
        cots[z, 32:64] = g2_ref[0, z]
        cots[z, 64:96] = g2_ref[1, z]
        cots[z, 96:128] = after_ref[0, z]
    sgrad = [None, None, None]
    tgrad = None
    bgrad = None
    for f in range(2):
        for p in range(4):
            plane = low_ref[f, 0] if p == 0 else high_ref[f, 0] if p == 3 else y1_ref[f, p - 1]
            for c in (-1, 0, 1):
                across = moved_cols(plane, c, col_of)
                for r in (-1, 0, 1):
                    at = p * WIN + (3 * (r + 1) + c + 1) * CH
                    columns[f, at : at + CH, :] = moved_rows(across, r)
        for z in range(2):
            pre = nn(weight, columns[f, z * WIN : (z + 3) * WIN, :]) + bias
            sigma = 1.0 / (1.0 + jnp.exp(-pre))
            active = (pre * sigma).astype(BF16)
            around = cots[z, f * CH : (f + 3) * CH, :]
            through = lax.dot_general(tback, around, (((0,), (0,)), ((), ())), preferred_element_type=F32)
            hgrad = (through * sigma * (1.0 + pre * (1.0 - sigma))).astype(BF16)
            active_ref[f, z] = active
            hgrad_ref[f, z] = hgrad
            tpart = nt(around, active)
            tgrad = tpart if tgrad is None else tgrad + tpart
            bpart = jnp.sum(hgrad.astype(F32), axis=1, keepdims=True)
            bgrad = bpart if bgrad is None else bgrad + bpart
            for dz in range(3):
                part = nt(hgrad, columns[f, (z + dz) * WIN : (z + dz + 1) * WIN, :])
                sgrad[dz] = part if sgrad[dz] is None else sgrad[dz] + part
    for dz in range(3):
        for half in range(2):
            at = (2 * dz + half) * HID
            pay_ref[at : at + HID, :] = sgrad[dz][:, half * 128 : (half + 1) * 128].astype(BF16)
    tail = jnp.concatenate(
        [sgrad[dz][:, 256:288] for dz in range(3)] + [jnp.broadcast_to(bgrad, (HID, CH))], axis=1
    )
    pay_ref[384:448, :] = tail.astype(BF16)
    pay_ref[448:480, :] = jnp.concatenate([tgrad[64:96], tgrad[32:64]], axis=1).astype(BF16)
    pay_ref[480:512, :] = jnp.concatenate([tgrad[0:32], jnp.zeros((32, 64), F32)], axis=1).astype(BF16)


def outputs_kernel(
    y2_ref, g1_ref, act_ref, before_ref, after_ref, hg_ref, low_ref, high_ref, sw_ref, tw_ref,
    rebuilt_ref, gin_ref,
    acts, hgs,
):
    col_of = lax.rem(lax.broadcasted_iota(jnp.int32, (CH, PIX), 1), COLS)
    tahead = jnp.concatenate([tw_ref[0], tw_ref[1], tw_ref[2]], axis=1)
    wback = jnp.concatenate([sw_ref[2], sw_ref[1], sw_ref[0]], axis=0)
    for z in range(2):
        acts[z, 0:64] = before_ref[0, z]
        acts[z, 64:128] = act_ref[0, z]
        acts[z, 128:192] = act_ref[1, z]
        acts[z, 192:256] = after_ref[0, z]
        for f in range(2):
            mapped = nn(tahead, acts[z, f * HID : (f + 3) * HID, :])
            rebuilt_ref[f, z] = (y2_ref[f, z].astype(F32) - mapped).astype(BF16)
    for f in range(2):
        hgs[f, 0:64] = low_ref[f, 0]
        hgs[f, 64:128] = hg_ref[f, 0]
        hgs[f, 128:192] = hg_ref[f, 1]
        hgs[f, 192:256] = high_ref[f, 0]
        for z in range(2):
            spread = lax.dot_general(
                wback, hgs[f, z * HID : (z + 3) * HID, :], (((0,), (0,)), ((), ())), preferred_element_type=F32
            )
            total = g1_ref[f, z].astype(F32)
            for c in (-1, 0, 1):
                lines = None
                for r in (-1, 0, 1):
                    at = (3 * (r + 1) + c + 1) * CH
                    part = moved_rows(spread[at : at + CH], -r)
                    lines = part if lines is None else lines + part
                total = total + moved_cols(lines, -c, col_of)
            gin_ref[f, z] = total.astype(BF16)


def grads_kernel(factor, got_ref, gs_ref, gb_ref, gt_ref):
    tail = got_ref[384:448, :].astype(F32) * factor
    for dz in range(3):
        at = 2 * dz * HID
        gs_ref[dz, :, 0:128] = got_ref[at : at + HID, :].astype(F32) * factor
        gs_ref[dz, :, 128:256] = got_ref[at + HID : at + 2 * HID, :].astype(F32) * factor
        gs_ref[dz, :, 256:288] = tail[:, dz * CH : (dz + 1) * CH]
    gb_ref[...] = tail[:, 96:128].T[0:1]
    taps = got_ref[448:512, :].astype(F32) * factor
    gt_ref[0] = taps[0:32, 0:64]
    gt_ref[1] = taps[0:32, 64:128]
    gt_ref[2] = taps[32:64, 0:64]


def whole(shape):
    return pl.BlockSpec(shape, lambda i: (0,) * len(shape))


def half(which):
    return pl.BlockSpec((2, 2, CH, PIX), lambda i: (0, 0, which, 0))


def shards(outputs_fwd, cotangent, spatial_weight, hidden_bias, temporal_weight):
    axes = ("gz", "ta")
    gz, ta = lax.axis_size("gz"), lax.axis_size("ta")
    up = [(i, i + 1) for i in range(gz - 1)]
    down = [(i + 1, i) for i in range(gz - 1)]
    later = [(i, (i + 1) % ta) for i in range(ta)]
    sooner = [((i + 1) % ta, i) for i in range(ta)]
    params = pltpu.CompilerParams(vmem_limit_bytes=VMEM_LIMIT)

    low = lax.ppermute(outputs_fwd[:, 1:2, :CH], "gz", up)
    high = lax.ppermute(outputs_fwd[:, 0:1, :CH], "gz", down)
    before = lax.ppermute(cotangent[1:2, :, CH:], "ta", later)
    after = lax.ppermute(cotangent[0:1, :, CH:], "ta", sooner)

    active, hgrad, pay = pl.pallas_call(
        hidden_kernel,
        grid=(1,),
        in_specs=[
            half(0), whole((2, 1, CH, PIX)), whole((2, 1, CH, PIX)),
            half(1), whole((1, 2, CH, PIX)), whole((1, 2, CH, PIX)),
            whole((3, HID, WIN)), whole((HID, 1)), whole((3, CH, HID)),
        ],
        out_specs=[whole((2, 2, HID, PIX)), whole((2, 2, HID, PIX)), whole((512, 128))],
        out_shape=[
            jax.ShapeDtypeStruct((2, 2, HID, PIX), BF16),
            jax.ShapeDtypeStruct((2, 2, HID, PIX), BF16),
            jax.ShapeDtypeStruct((512, 128), BF16),
        ],
        scratch_shapes=[pltpu.VMEM((2, 4 * WIN, PIX), BF16), pltpu.VMEM((2, 4 * CH, PIX), BF16)],
        compiler_params=params,
        cost_estimate=pl.CostEstimate(flops=10**9, bytes_accessed=4 * 10**6, transcendentals=0),
        name="hidden",
    )(outputs_fwd, low, high, cotangent, before, after, spatial_weight, hidden_bias.reshape(HID, 1), temporal_weight)

    parts = lax.all_to_all(pay.reshape(256, 2, 128), axes, 0, 0)
    summed = jnp.sum(parts.astype(F32), axis=0).astype(BF16)
    got = lax.all_to_all(jnp.broadcast_to(summed[None], (256, 2, 128)), axes, 0, 0)

    act_before = lax.ppermute(active[1:2], "ta", later)
    act_after = lax.ppermute(active[0:1], "ta", sooner)
    hg_low = lax.ppermute(hgrad[:, 1:2], "gz", up)
    hg_high = lax.ppermute(hgrad[:, 0:1], "gz", down)

    rebuilt, grad_in = pl.pallas_call(
        outputs_kernel,
        grid=(1,),
        in_specs=[
            half(1), half(0),
            whole((2, 2, HID, PIX)), whole((1, 2, HID, PIX)), whole((1, 2, HID, PIX)),
            whole((2, 2, HID, PIX)), whole((2, 1, HID, PIX)), whole((2, 1, HID, PIX)),
            whole((3, HID, WIN)), whole((3, CH, HID)),
        ],
        out_specs=[whole((2, 2, CH, PIX)), whole((2, 2, CH, PIX))],
        out_shape=[jax.ShapeDtypeStruct((2, 2, CH, PIX), BF16)] * 2,
        scratch_shapes=[pltpu.VMEM((2, 4 * HID, PIX), BF16), pltpu.VMEM((2, 4 * HID, PIX), BF16)],
        compiler_params=params,
        cost_estimate=pl.CostEstimate(flops=10**9, bytes_accessed=4 * 10**6, transcendentals=0),
        name="outputs",
    )(outputs_fwd, cotangent, active, act_before, act_after, hgrad, hg_low, hg_high, spatial_weight, temporal_weight)

    factor = 1.0 / math.sqrt(2 * ta * 2 * gz * PIX)
    grad_spatial, grad_bias, grad_temporal = pl.pallas_call(
        lambda *refs: grads_kernel(factor, *refs),
        out_shape=[
            jax.ShapeDtypeStruct((3, HID, WIN), F32),
            jax.ShapeDtypeStruct((1, HID), F32),
            jax.ShapeDtypeStruct((3, CH, HID), F32),
        ],
        name="grads",
    )(got.reshape(512, 128))
    return rebuilt, grad_in, grad_spatial, grad_bias.reshape(HID), grad_temporal


def solution(mesh):
    placed = P("ta", "gz", None, None)
    return jax.shard_map(
        shards,
        mesh=mesh,
        in_specs=(placed, placed, P(), P(), P()),
        out_specs=(placed, placed, P(), P(), P()),
        check_vma=False,
    )
```

```python
import math

import jax
import jax.numpy as jnp
from jax import lax
from jax.experimental import pallas as pl
from jax.experimental.pallas import tpu as pltpu
from jax.sharding import PartitionSpec as P

ROWS = 8
COLS = 160
PIX = ROWS * COLS
CH = 32
HID = 64
WIN = 9 * CH
F32 = jnp.float32
BF16 = jnp.bfloat16
VMEM_LIMIT = 24 * 1024 * 1024
GZ = ("yl", "z", "c")
TA = ("yh", "x")
FLAT = ("yl", "yh", "x", "c")
LONG = pl.CostEstimate(flops=2 * 10**9, bytes_accessed=4 * 10**6, transcendentals=0)
PARAMS = pltpu.CompilerParams(vmem_limit_bytes=VMEM_LIMIT)
IN_VMEM = pl.BlockSpec(memory_space=pltpu.VMEM)
ANYWHERE = pl.BlockSpec(memory_space=pl.ANY)
IN_HBM = pl.BlockSpec(memory_space=pltpu.HBM)


def nn(a, b):
    return lax.dot_general(a, b, (((1,), (0,)), ((), ())), preferred_element_type=F32)


def nt(a, b):
    return lax.dot_general(a, b, (((1,), (1,)), ((), ())), preferred_element_type=F32)


def tn(a, b):
    return lax.dot_general(a, b, (((0,), (0,)), ((), ())), preferred_element_type=F32)


def moved_rows(field, rows):
    if rows == 0:
        return field
    edge = jnp.zeros((field.shape[0], COLS), field.dtype)
    if rows > 0:
        return jnp.concatenate([field[:, COLS:], edge], axis=1)
    return jnp.concatenate([edge, field[:, : PIX - COLS]], axis=1)


def moved_cols(field, cols, col_of):
    if cols == 0:
        return field
    rolled = pltpu.roll(field, (-cols) % PIX, 1)
    return jnp.where(col_of == (COLS - 1 if cols > 0 else 0), jnp.zeros_like(rolled), rolled)


def parities():
    return lax.axis_index("c"), lax.rem(lax.axis_index("x"), 2)


def edges_kernel(fwd_ref, cot_ref, odd_ref, even_ref, far_ref, near_ref, sems):
    core, odd = parities()
    copies = [
        pltpu.make_async_copy(cot_ref.at[pl.ds(odd, 1), :, CH : 2 * CH], odd_ref, sems.at[0]),
        pltpu.make_async_copy(cot_ref.at[pl.ds(1 - odd, 1), :, CH : 2 * CH], even_ref, sems.at[1]),
        pltpu.make_async_copy(fwd_ref.at[:, pl.ds(core, 1), 0:CH], far_ref, sems.at[2]),
        pltpu.make_async_copy(fwd_ref.at[:, pl.ds(1 - core, 1), 0:CH], near_ref, sems.at[3]),
    ]
    for copy in copies:
        copy.start()
    for copy in copies:
        copy.wait()


def hidden_kernel(
    odd_ref, even_ref, far_ref, near_ref, fwd_ref, cot_ref, weight_ref, bias_ref, tw_ref,
    active_ref, hgrad_ref, pay_ref,
    columns, cots,
):
    core, odd = parities()
    col_of = lax.rem(lax.broadcasted_iota(jnp.int32, (CH, PIX), 1), COLS)
    weight = weight_ref[...]
    bias = bias_ref[...]
    tback = jnp.concatenate([tw_ref[2], tw_ref[1], tw_ref[0]], axis=0)
    for z in range(2):
        cots[z, 0:32] = jnp.where(odd == 0, odd_ref[0, z], even_ref[0, z])
        cots[z, 32:64] = cot_ref[0, z, CH : 2 * CH]
        cots[z, 64:96] = cot_ref[1, z, CH : 2 * CH]
        cots[z, 96:128] = jnp.where(odd == 0, even_ref[0, z], odd_ref[0, z])
    sgrad = [None, None, None]
    tgrad = None
    bgrad = None
    for f in range(2):
        low = jnp.where(core == 0, far_ref[f, 0], near_ref[f, 0])
        high = jnp.where(core == 0, near_ref[f, 0], far_ref[f, 0])
        for p in range(4):
            plane = low if p == 0 else high if p == 3 else fwd_ref[f, p - 1, 0:CH]
            for c in (-1, 0, 1):
                across = moved_cols(plane, c, col_of)
                for r in (-1, 0, 1):
                    at = p * WIN + (3 * (r + 1) + c + 1) * CH
                    columns[f, at : at + CH, :] = moved_rows(across, r)
        for z in range(2):
            pre = nn(weight, columns[f, z * WIN : (z + 3) * WIN, :]) + bias
            sigma = 1.0 / (1.0 + jnp.exp(-pre))
            active = (pre * sigma).astype(BF16)
            around = cots[z, f * CH : (f + 3) * CH, :]
            through = tn(tback, around)
            hgrad = (through * sigma * (1.0 + pre * (1.0 - sigma))).astype(BF16)
            active_ref[f, z] = active
            hgrad_ref[f, z] = hgrad
            tpart = nt(around, active)
            tgrad = tpart if tgrad is None else tgrad + tpart
            bpart = jnp.sum(hgrad.astype(F32), axis=1, keepdims=True)
            bgrad = bpart if bgrad is None else bgrad + bpart
            for dz in range(3):
                part = nt(hgrad, columns[f, (z + dz) * WIN : (z + dz + 1) * WIN, :])
                sgrad[dz] = part if sgrad[dz] is None else sgrad[dz] + part
    for dz in range(3):
        for side in range(2):
            at = (2 * dz + side) * HID
            pay_ref[at : at + HID, :] = sgrad[dz][:, side * 128 : (side + 1) * 128].astype(BF16)
    bhigh, blow = two_parts(bgrad)
    pay_ref[384:448, :] = jnp.concatenate(
        [sgrad[dz][:, 256:288].astype(BF16) for dz in range(3)]
        + [jnp.broadcast_to(bhigh, (HID, 16)), jnp.broadcast_to(blow, (HID, 16))],
        axis=1,
    )
    pay_ref[448:480, :] = jnp.concatenate([tgrad[64:96], tgrad[32:64]], axis=1).astype(BF16)
    pay_ref[480:512, :] = jnp.concatenate([tgrad[0:32], jnp.zeros((32, 64), F32)], axis=1).astype(BF16)


def two_parts(value):
    high = value.astype(BF16)
    return high, (value - high.astype(F32)).astype(BF16)


def sum_kernel(count, got_ref, out_ref):
    rank = ((lax.axis_index("yl") * 2 + lax.axis_index("yh")) * 4 + lax.axis_index("x")) * 2 + lax.axis_index("c")
    total = got_ref[0].astype(F32)
    for i in range(1, got_ref.shape[0]):
        total = total + got_ref[i].astype(F32)
    both = total[:, 96:112] + total[:, 112:128]
    high, low = two_parts(both)
    split = jnp.concatenate([total[:, 0:96].astype(BF16), high, low], axis=1)
    has_bias = jnp.logical_and(rank >= 24, rank < 28)
    out = jnp.where(has_bias, split, total.astype(BF16))
    for i in range(count):
        out_ref[i] = out


def own_kernel(
    act_ref, hg_ref, sw_ref, tw_ref,
    mapped_ref, gin_ref, odd_ref, even_ref, far_ref, near_ref,
):
    core, odd = parities()
    col_of = lax.rem(lax.broadcasted_iota(jnp.int32, (CH, PIX), 1), COLS)
    none = jnp.zeros((CH, HID), BF16)
    ahead = jnp.concatenate(
        [
            jnp.concatenate([tw_ref[2], none], axis=1),
            jnp.concatenate([tw_ref[1], tw_ref[2]], axis=1),
            jnp.concatenate([tw_ref[0], tw_ref[1]], axis=1),
            jnp.concatenate([none, tw_ref[0]], axis=1),
        ],
        axis=0,
    )
    for z in range(2):
        mapped = nn(ahead, jnp.concatenate([act_ref[0, z], act_ref[1, z]], axis=0))
        for f in range(2):
            mapped_ref[f, z] = mapped[(f + 1) * CH : (f + 2) * CH]
        sooner, later = mapped[0:CH], mapped[3 * CH : 4 * CH]
        odd_ref[0, z] = jnp.where(odd == 0, sooner, later).astype(BF16)
        even_ref[0, z] = jnp.where(odd == 0, later, sooner).astype(BF16)

    def gathered(spread):
        total = None
        for c in (-1, 0, 1):
            lines = None
            for r in (-1, 0, 1):
                at = (3 * (r + 1) + c + 1) * CH
                part = moved_rows(spread[at : at + CH], -r)
                lines = part if lines is None else lines + part
            lines = moved_cols(lines, -c, col_of)
            total = lines if total is None else total + lines
        return total

    upper = jnp.concatenate([sw_ref[1], sw_ref[0]], axis=0)
    lower = jnp.concatenate([sw_ref[2], sw_ref[1]], axis=0)
    for f in range(2):
        both = jnp.concatenate([hg_ref[f, 0], hg_ref[f, 1]], axis=0)
        below = gathered(tn(sw_ref[0], hg_ref[f, 0]))
        above = gathered(tn(sw_ref[2], hg_ref[f, 1]))
        far_ref[f, 0] = jnp.where(core == 0, below, above).astype(BF16)
        near_ref[f, 0] = jnp.where(core == 0, above, below).astype(BF16)
        gin_ref[f, 0] = gathered(tn(upper, both))
        gin_ref[f, 1] = gathered(tn(lower, both))


def outputs_kernel(
    odd_ref, even_ref, far_ref, near_ref, mapped_ref, gpart_ref, fwd_ref, cot_ref, rebuilt_ref, gin_ref
):
    core, odd = parities()
    for f in range(2):
        for z in range(2):
            beside = jnp.where(odd == f, odd_ref[0, z], even_ref[0, z])
            mapped = mapped_ref[f, z] + beside.astype(F32)
            rebuilt_ref[f, z] = (fwd_ref[f, z, CH : 2 * CH].astype(F32) - mapped).astype(BF16)
            beside = jnp.where(core == z, far_ref[f, 0], near_ref[f, 0])
            back = gpart_ref[f, z] + beside.astype(F32)
            gin_ref[f, z] = (cot_ref[f, z, 0:CH].astype(F32) + back).astype(BF16)


def grads_kernel(factor, got_ref, gs_ref, gb_ref, gt_ref):
    tail = got_ref[384:448, :].astype(F32) * factor
    for dz in range(3):
        at = 2 * dz * HID
        gs_ref[dz, :, 0:128] = got_ref[at : at + HID, :].astype(F32) * factor
        gs_ref[dz, :, 128:256] = got_ref[at + HID : at + 2 * HID, :].astype(F32) * factor
        gs_ref[dz, :, 256:288] = tail[:, dz * CH : (dz + 1) * CH]
    gb_ref[...] = (tail[:, 96:112] + tail[:, 112:128]).T[0:1]
    taps = got_ref[448:512, :].astype(F32) * factor
    gt_ref[0] = taps[0:32, 0:64]
    gt_ref[1] = taps[0:32, 64:128]
    gt_ref[2] = taps[32:64, 0:64]


def shaped(*dims, dtype=BF16):
    return jax.ShapeDtypeStruct(dims, dtype)


def swaps(pairs):
    return [(a, b) for a, b in pairs] + [(b, a) for a, b in pairs]


def total_of(parts, count, name):
    return pl.pallas_call(
        lambda *refs: sum_kernel(count, *refs),
        in_specs=[IN_VMEM],
        out_specs=IN_VMEM,
        out_shape=shaped(count, 16, 128),
        compiler_params=PARAMS,
        cost_estimate=LONG,
        name=name,
    )(parts)


def shards(outputs_fwd, cotangent, spatial_weight, hidden_bias, temporal_weight):
    gz, ta = lax.axis_size(GZ), lax.axis_size(TA)
    to_far = swaps([(i, i + 1) for i in range(1, gz - 1, 2)])
    to_near = swaps([(i, i + 1) for i in range(0, gz, 2)])
    to_even = swaps([(i, i + 1) for i in range(0, ta, 2)])
    to_odd = swaps([(i, (i + 1) % ta) for i in range(1, ta, 2)])

    g2_odd, g2_even, y1_far, y1_near = pl.pallas_call(
        edges_kernel,
        in_specs=[IN_HBM] * 2,
        out_specs=[ANYWHERE] * 4,
        out_shape=[shaped(1, 2, CH, PIX)] * 2 + [shaped(2, 1, CH, PIX)] * 2,
        scratch_shapes=[pltpu.SemaphoreType.DMA((4,))],
        compiler_params=pltpu.CompilerParams(vmem_limit_bytes=54200 * 1024),
        name="edges",
    )(outputs_fwd, cotangent)
    g2_odd = lax.ppermute(g2_odd, TA, to_odd)
    g2_even = lax.ppermute(g2_even, TA, to_even)
    y1_far = lax.ppermute(y1_far, GZ, to_far)
    y1_near = lax.ppermute(y1_near, GZ, to_near)

    weight = jnp.concatenate([spatial_weight[0], spatial_weight[1], spatial_weight[2]], axis=1)
    active, hgrad, pay = pl.pallas_call(
        hidden_kernel,
        in_specs=[IN_VMEM] * 9,
        out_specs=[IN_VMEM] * 3,
        out_shape=[shaped(2, 2, HID, PIX)] * 2 + [shaped(512, 128)],
        scratch_shapes=[pltpu.VMEM((2, 4 * WIN, PIX), BF16), pltpu.VMEM((2, 4 * CH, PIX), BF16)],
        compiler_params=PARAMS,
        cost_estimate=pl.CostEstimate(flops=10**9, bytes_accessed=4 * 10**6, transcendentals=0),
        name="hidden",
    )(g2_odd, g2_even, y1_far, y1_near, outputs_fwd, cotangent, weight, hidden_bias.reshape(HID, 1), temporal_weight)

    parts = lax.all_to_all(pay.reshape(32, 16, 128), FLAT, 0, 0)
    mapped_own, gin_own, map_odd, map_even, gin_far, gin_near = pl.pallas_call(
        own_kernel,
        in_specs=[IN_VMEM] * 4,
        out_specs=[IN_VMEM] * 6,
        out_shape=[shaped(2, 2, CH, PIX, dtype=F32)] * 2
        + [shaped(1, 2, CH, PIX)] * 2
        + [shaped(2, 1, CH, PIX)] * 2,
        compiler_params=PARAMS,
        cost_estimate=LONG,
        name="own",
    )(active, hgrad, spatial_weight, temporal_weight)
    parts, map_odd, map_even, gin_far, gin_near = lax.optimization_barrier(
        (parts, map_odd, map_even, gin_far, gin_near)
    )
    parts = lax.all_to_all(total_of(parts, 8, "plane_sums"), "z", 0, 0)
    got = lax.all_to_all(total_of(parts, 32, "all_sums"), FLAT, 0, 0)

    map_odd = lax.ppermute(map_odd, TA, to_odd)
    map_even = lax.ppermute(map_even, TA, to_even)
    gin_far = lax.ppermute(gin_far, GZ, to_far)
    gin_near = lax.ppermute(gin_near, GZ, to_near)

    rebuilt, grad_in = pl.pallas_call(
        outputs_kernel,
        in_specs=[IN_VMEM] * 8,
        out_specs=[IN_VMEM] * 2,
        out_shape=[shaped(2, 2, CH, PIX)] * 2,
        compiler_params=PARAMS,
        cost_estimate=LONG,
        name="outputs",
    )(map_odd, map_even, gin_far, gin_near, mapped_own, gin_own, outputs_fwd, cotangent)
    got, rebuilt, grad_in = lax.optimization_barrier((got, rebuilt, grad_in))

    factor = 1.0 / math.sqrt(2 * ta * 2 * gz * PIX)
    grad_spatial, grad_bias, grad_temporal = pl.pallas_call(
        lambda *refs: grads_kernel(factor, *refs),
        in_specs=[IN_VMEM],
        out_specs=[IN_VMEM] * 3,
        out_shape=[shaped(3, HID, WIN, dtype=F32), shaped(1, HID, dtype=F32), shaped(3, CH, HID, dtype=F32)],
        compiler_params=PARAMS,
        name="grads",
    )(got.reshape(512, 128))
    return rebuilt, grad_in, grad_spatial, grad_bias.reshape(HID), grad_temporal


def solution(mesh):
    fine = jax.sharding.Mesh(mesh.devices.reshape(2, 8, 2, 2, 4), ("yl", "z", "c", "yh", "x"))
    placed = P(TA, GZ, None, None)
    return jax.shard_map(
        shards,
        mesh=fine,
        in_specs=(placed, placed, P(), P(), P()),
        out_specs=(placed, placed, P(), P(), P()),
        check_vma=False,
    )
```

```python
import math

import jax
import jax.numpy as jnp
from jax import lax
from jax.experimental import pallas as pl
from jax.experimental.pallas import tpu as pltpu
from jax.sharding import PartitionSpec as P

ROWS = 8
COLS = 160
PIX = ROWS * COLS
CH = 32
HID = 64
WIN = 9 * CH
F32 = jnp.float32
BF16 = jnp.bfloat16
VMEM_LIMIT = 24 * 1024 * 1024
EDGES_KIB = 54200
LATE_KIB = 54600
LAST_KIB = 54000
OWN_KIB = 24000
GZ = ("yl", "z", "c")
TA = ("yh", "x")
FLAT = ("yl", "yh", "x", "c")
LONG = pl.CostEstimate(flops=2 * 10**9, bytes_accessed=4 * 10**6, transcendentals=0)
PARAMS = pltpu.CompilerParams(vmem_limit_bytes=VMEM_LIMIT)
IN_VMEM = pl.BlockSpec(memory_space=pltpu.VMEM)
ANYWHERE = pl.BlockSpec(memory_space=pl.ANY)
IN_HBM = pl.BlockSpec(memory_space=pltpu.HBM)


def nn(a, b):
    return lax.dot_general(a, b, (((1,), (0,)), ((), ())), preferred_element_type=F32)


def nt(a, b):
    return lax.dot_general(a, b, (((1,), (1,)), ((), ())), preferred_element_type=F32)


def tn(a, b):
    return lax.dot_general(a, b, (((0,), (0,)), ((), ())), preferred_element_type=F32)


def moved_rows(field, rows):
    if rows == 0:
        return field
    edge = jnp.zeros((field.shape[0], COLS), field.dtype)
    if rows > 0:
        return jnp.concatenate([field[:, COLS:], edge], axis=1)
    return jnp.concatenate([edge, field[:, : PIX - COLS]], axis=1)


def moved_cols(field, cols, col_of):
    if cols == 0:
        return field
    rolled = pltpu.roll(field, (-cols) % PIX, 1)
    return jnp.where(col_of == (COLS - 1 if cols > 0 else 0), jnp.zeros_like(rolled), rolled)


def parities():
    return lax.axis_index("c"), lax.rem(lax.axis_index("x"), 2)


def edges_kernel(fwd_ref, cot_ref, odd_ref, even_ref, far_ref, near_ref, sems):
    core, odd = parities()
    copies = [
        pltpu.make_async_copy(cot_ref.at[pl.ds(odd, 1), :, CH : 2 * CH], odd_ref, sems.at[0]),
        pltpu.make_async_copy(cot_ref.at[pl.ds(1 - odd, 1), :, CH : 2 * CH], even_ref, sems.at[1]),
        pltpu.make_async_copy(fwd_ref.at[:, pl.ds(core, 1), 0:CH], far_ref, sems.at[2]),
        pltpu.make_async_copy(fwd_ref.at[:, pl.ds(1 - core, 1), 0:CH], near_ref, sems.at[3]),
    ]
    for copy in copies:
        copy.start()
    for copy in copies:
        copy.wait()


def weights_kernel(sw_ref, bias_ref, tw_ref, weight_ref, bias_out_ref, tback_ref):
    weight_ref[...] = jnp.concatenate([sw_ref[0], sw_ref[1], sw_ref[2]], axis=1)
    bias_out_ref[...] = jnp.broadcast_to(bias_ref[...], (8, HID)).T[:, 0:1]
    for k in range(3):
        tback_ref[k * CH : (k + 1) * CH] = tw_ref[2 - k]


def hidden_kernel(
    odd_ref, even_ref, far_ref, near_ref, fwd_ref, cot_ref, weight_ref, bias_ref, tback_ref,
    active_ref, hgrad_ref, pay_ref,
    columns, cots,
):
    core, odd = parities()
    col_of = lax.rem(lax.broadcasted_iota(jnp.int32, (CH, PIX), 1), COLS)
    weight = weight_ref[...]
    bias = bias_ref[...]
    tback = tback_ref[...]
    for z in range(2):
        cots[z, 0:32] = jnp.where(odd == 0, odd_ref[0, z], even_ref[0, z])
        cots[z, 32:64] = cot_ref[0, z, CH : 2 * CH]
        cots[z, 64:96] = cot_ref[1, z, CH : 2 * CH]
        cots[z, 96:128] = jnp.where(odd == 0, even_ref[0, z], odd_ref[0, z])
    sgrad = [None, None, None]
    tgrad = None
    bgrad = None

    def unfold(f, p, plane):
        for c in (-1, 0, 1):
            across = moved_cols(plane, c, col_of)
            for r in (-1, 0, 1):
                at = p * WIN + (3 * (r + 1) + c + 1) * CH
                columns[f, at : at + CH, :] = moved_rows(across, r)

    for f in range(2):
        unfold(f, 0, jnp.where(core == 0, far_ref[f, 0], near_ref[f, 0]))
        unfold(f, 1, fwd_ref[f, 0, 0:CH])
        unfold(f, 2, fwd_ref[f, 1, 0:CH])
        unfold(f, 3, jnp.where(core == 0, near_ref[f, 0], far_ref[f, 0]))
        for z in range(2):
            pre = nn(weight, columns[f, z * WIN : (z + 3) * WIN, :]) + bias
            sigma = 1.0 / (1.0 + jnp.exp(-pre))
            active = (pre * sigma).astype(BF16)
            around = cots[z, f * CH : (f + 3) * CH, :]
            through = tn(tback, around)
            hgrad = (through * sigma * (1.0 + pre * (1.0 - sigma))).astype(BF16)
            active_ref[f, z] = active
            hgrad_ref[f, z] = hgrad
            tpart = nt(around, active)
            tgrad = tpart if tgrad is None else tgrad + tpart
            bpart = jnp.sum(hgrad.astype(F32), axis=1, keepdims=True)
            bgrad = bpart if bgrad is None else bgrad + bpart
            for dz in range(3):
                part = nt(hgrad, columns[f, (z + dz) * WIN : (z + dz + 1) * WIN, :])
                sgrad[dz] = part if sgrad[dz] is None else sgrad[dz] + part
    for dz in range(3):
        for side in range(2):
            at = (2 * dz + side) * HID
            pay_ref[at : at + HID, :] = sgrad[dz][:, side * 128 : (side + 1) * 128].astype(BF16)
    bhigh, blow = two_parts(bgrad)
    pay_ref[384:448, :] = jnp.concatenate(
        [sgrad[dz][:, 256:288].astype(BF16) for dz in range(3)]
        + [jnp.broadcast_to(bhigh, (HID, 16)), jnp.broadcast_to(blow, (HID, 16))],
        axis=1,
    )
    pay_ref[448:480, :] = jnp.concatenate([tgrad[64:96], tgrad[32:64]], axis=1).astype(BF16)
    pay_ref[480:512, :] = jnp.concatenate([tgrad[0:32], jnp.zeros((32, 64), F32)], axis=1).astype(BF16)


def two_parts(value):
    high = value.astype(BF16)
    return high, (value - high.astype(F32)).astype(BF16)


def sum_kernel(count, got_ref, out_ref):
    rank = ((lax.axis_index("yl") * 2 + lax.axis_index("yh")) * 4 + lax.axis_index("x")) * 2 + lax.axis_index("c")
    total = got_ref[0].astype(F32)
    for i in range(1, got_ref.shape[0]):
        total = total + got_ref[i].astype(F32)
    both = total[:, 96:112] + total[:, 112:128]
    high, low = two_parts(both)
    split = jnp.concatenate([total[:, 0:96].astype(BF16), high, low], axis=1)
    has_bias = jnp.logical_and(rank >= 24, rank < 28)
    out = jnp.where(has_bias, split, total.astype(BF16))
    for i in range(count):
        out_ref[i] = out


def own_kernel(
    act_ref, hg_ref, sw_ref, tw_ref,
    mapped_ref, gin_ref, odd_ref, even_ref, far_ref, near_ref,
):
    core, odd = parities()
    none = jnp.zeros((CH, HID), BF16)
    ahead = jnp.concatenate(
        [
            jnp.concatenate([tw_ref[2], none], axis=1),
            jnp.concatenate([tw_ref[1], tw_ref[2]], axis=1),
            jnp.concatenate([tw_ref[0], tw_ref[1]], axis=1),
            jnp.concatenate([none, tw_ref[0]], axis=1),
        ],
        axis=0,
    )
    for z in range(2):
        mapped = nn(ahead, jnp.concatenate([act_ref[0, z], act_ref[1, z]], axis=0))
        for f in range(2):
            mapped_ref[f, z] = mapped[(f + 1) * CH : (f + 2) * CH]
        sooner, later = mapped[0:CH], mapped[3 * CH : 4 * CH]
        odd_ref[0, z] = jnp.where(odd == 0, sooner, later).astype(BF16)
        even_ref[0, z] = jnp.where(odd == 0, later, sooner).astype(BF16)

    back = jnp.concatenate(
        [
            jnp.concatenate(
                [sw_ref[dz, :, (3 * r + c) * CH : (3 * r + c + 1) * CH] for dz in range(3) for r in range(3)], axis=1
            )
            for c in range(3)
        ],
        axis=0,
    )
    col_of = lax.rem(lax.broadcasted_iota(jnp.int32, (HID, PIX), 1), COLS)

    def rows_joined(lines):
        return lines[CH : 2 * CH] + moved_rows(lines[0:CH], 1) + moved_rows(lines[2 * CH : 3 * CH], -1)

    for f in range(2):
        spread = []
        for z in range(2):
            field = hg_ref[f, z]
            spread.append(tn(back, jnp.concatenate([moved_cols(field, -c, col_of) for c in (-1, 0, 1)], axis=0)))
        below = rows_joined(spread[0][0:96])
        above = rows_joined(spread[1][192:288])
        gin_ref[f, 0] = rows_joined(spread[0][96:192] + spread[1][0:96])
        gin_ref[f, 1] = rows_joined(spread[0][192:288] + spread[1][96:192])
        far_ref[f, 0] = jnp.where(core == 0, below, above).astype(BF16)
        near_ref[f, 0] = jnp.where(core == 0, above, below).astype(BF16)


def rebuilt_kernel(seam_ref, inner_ref, even_ref, mapped_ref, fwd_ref, rebuilt_ref):
    odd = parities()[1]
    place = lax.axis_index("x")
    seam = jnp.logical_or(place == 0, place == lax.axis_size("x") - 1)
    for z in range(2):
        from_odd = jnp.where(seam, seam_ref[0, z], inner_ref[0, z])
        for f in range(2):
            beside = jnp.where(odd == f, from_odd, even_ref[0, z])
            mapped = mapped_ref[f, z] + beside.astype(F32)
            rebuilt_ref[f, z] = (fwd_ref[f, z, CH : 2 * CH].astype(F32) - mapped).astype(BF16)


def gin_kernel(far_ref, near_ref, own_ref, cot_ref, gin_ref):
    core = parities()[0]
    for f in range(2):
        for z in range(2):
            beside = jnp.where(core == z, far_ref[f, 0], near_ref[f, 0])
            back = own_ref[f, z] + beside.astype(F32)
            gin_ref[f, z] = (cot_ref[f, z, 0:CH].astype(F32) + back).astype(BF16)


def grads_kernel(factor, got_ref, gs_ref, gb_ref, gt_ref):
    tail = got_ref[384:448, :].astype(F32) * factor
    for dz in range(3):
        at = 2 * dz * HID
        gs_ref[dz, :, 0:128] = got_ref[at : at + HID, :].astype(F32) * factor
        gs_ref[dz, :, 128:256] = got_ref[at + HID : at + 2 * HID, :].astype(F32) * factor
        gs_ref[dz, :, 256:288] = tail[:, dz * CH : (dz + 1) * CH]
    gb_ref[...] = (tail[:, 96:112] + tail[:, 112:128]).T[0:1]
    taps = got_ref[448:512, :].astype(F32) * factor
    gt_ref[0] = taps[0:32, 0:64]
    gt_ref[1] = taps[0:32, 64:128]
    gt_ref[2] = taps[32:64, 0:64]


def shaped(*dims, dtype=BF16):
    return jax.ShapeDtypeStruct(dims, dtype)


def swaps(pairs):
    return [(a, b) for a, b in pairs] + [(b, a) for a, b in pairs]


def total_of(parts, count, name):
    return pl.pallas_call(
        lambda *refs: sum_kernel(count, *refs),
        in_specs=[IN_VMEM],
        out_specs=IN_VMEM,
        out_shape=shaped(count, 16, 128),
        compiler_params=PARAMS,
        cost_estimate=LONG,
        name=name,
    )(parts)


def finished(kernel, name, operands, kib, cost):
    return pl.pallas_call(
        kernel,
        in_specs=[IN_VMEM] * len(operands),
        out_specs=IN_VMEM,
        out_shape=shaped(2, 2, CH, PIX),
        compiler_params=pltpu.CompilerParams(vmem_limit_bytes=kib * 1024),
        cost_estimate=cost,
        name=name,
    )(*operands)


def shards(outputs_fwd, cotangent, spatial_weight, hidden_bias, temporal_weight):
    gz, ta = lax.axis_size(GZ), lax.axis_size(TA)
    to_far = swaps([(i, i + 1) for i in range(1, gz - 1, 2)])
    to_near = swaps([(i, i + 1) for i in range(0, gz, 2)])
    to_even = swaps([(i, i + 1) for i in range(0, ta, 2)])
    to_odd = swaps([(i, (i + 1) % ta) for i in range(1, ta, 2)])
    row = lax.axis_size("x")
    to_inner = swaps([(i, i + 1) for i in range(1, ta, 2) if (i + 1) % row])
    to_seam = swaps([(i, (i + 1) % ta) for i in range(1, ta, 2) if (i + 1) % row == 0])

    g2_odd, g2_even, y1_far, y1_near = pl.pallas_call(
        edges_kernel,
        in_specs=[IN_HBM] * 2,
        out_specs=[ANYWHERE] * 4,
        out_shape=[shaped(1, 2, CH, PIX)] * 2 + [shaped(2, 1, CH, PIX)] * 2,
        scratch_shapes=[pltpu.SemaphoreType.DMA((4,))],
        compiler_params=pltpu.CompilerParams(vmem_limit_bytes=EDGES_KIB * 1024),
        cost_estimate=pl.CostEstimate(flops=4 * 10**9, bytes_accessed=10**6, transcendentals=0),
        name="edges",
    )(outputs_fwd, cotangent)
    weight, bias, tback = pl.pallas_call(
        weights_kernel,
        in_specs=[IN_VMEM] * 3,
        out_specs=[IN_VMEM] * 3,
        out_shape=[shaped(HID, 3 * WIN), shaped(HID, 1, dtype=F32), shaped(3 * CH, HID)],
        compiler_params=PARAMS,
        name="weights",
    )(spatial_weight, hidden_bias.reshape(1, HID), temporal_weight)
    g2_odd = lax.ppermute(g2_odd, TA, to_odd)
    g2_even = lax.ppermute(g2_even, TA, to_even)
    y1_far = lax.ppermute(y1_far, GZ, to_far)
    y1_near = lax.ppermute(y1_near, GZ, to_near)

    active, hgrad, pay = pl.pallas_call(
        hidden_kernel,
        in_specs=[IN_VMEM] * 9,
        out_specs=[IN_VMEM] * 3,
        out_shape=[shaped(2, 2, HID, PIX)] * 2 + [shaped(512, 128)],
        scratch_shapes=[
            pltpu.VMEM((2, 4 * WIN, PIX), BF16),
            pltpu.VMEM((2, 4 * CH, PIX), BF16),
        ],
        compiler_params=PARAMS,
        cost_estimate=pl.CostEstimate(flops=10**9, bytes_accessed=4 * 10**6, transcendentals=0),
        name="hidden",
    )(g2_odd, g2_even, y1_far, y1_near, outputs_fwd, cotangent, weight, bias, tback)

    parts = lax.all_to_all(pay.reshape(32, 16, 128), FLAT, 0, 0)
    mapped_own, gin_own, map_odd, map_even, gin_far, gin_near = pl.pallas_call(
        own_kernel,
        in_specs=[IN_VMEM] * 4,
        out_specs=[IN_VMEM] * 6,
        out_shape=[shaped(2, 2, CH, PIX, dtype=F32)] * 2
        + [shaped(1, 2, CH, PIX)] * 2
        + [shaped(2, 1, CH, PIX)] * 2,
        compiler_params=pltpu.CompilerParams(vmem_limit_bytes=OWN_KIB * 1024),
        cost_estimate=LONG,
        name="own",
    )(active, hgrad, spatial_weight, temporal_weight)
    map_even = lax.ppermute(map_even, TA, to_even)
    map_inner = lax.ppermute(map_odd, TA, to_inner)
    parts, map_odd = lax.optimization_barrier((parts, map_odd))
    parts = lax.all_to_all(total_of(parts, 8, "plane_sums"), "z", 0, 0)
    map_seam = lax.ppermute(map_odd, TA, to_seam)
    parts, gin_far, gin_near = lax.optimization_barrier((parts, gin_far, gin_near))
    got = lax.all_to_all(total_of(parts, 32, "all_sums"), FLAT, 0, 0)
    rebuilt = finished(
        rebuilt_kernel, "rebuilt", (map_seam, map_inner, map_even, mapped_own, outputs_fwd), LATE_KIB, LONG
    )
    gin_far = lax.ppermute(gin_far, GZ, to_far)
    gin_near = lax.ppermute(gin_near, GZ, to_near)

    got, rebuilt = lax.optimization_barrier((got, rebuilt))

    factor = 1.0 / math.sqrt(2 * ta * 2 * gz * PIX)
    grad_spatial, grad_bias, grad_temporal = pl.pallas_call(
        lambda *refs: grads_kernel(factor, *refs),
        in_specs=[IN_VMEM],
        out_specs=[IN_VMEM] * 3,
        out_shape=[shaped(3, HID, WIN, dtype=F32), shaped(1, HID, dtype=F32), shaped(3, CH, HID, dtype=F32)],
        compiler_params=PARAMS,
        cost_estimate=LONG,
        name="grads",
    )(got.reshape(512, 128))
    gin_own, grad_spatial = lax.optimization_barrier((gin_own, grad_spatial))
    grad_in = finished(gin_kernel, "grad_in", (gin_far, gin_near, gin_own, cotangent), LAST_KIB, LONG)
    return rebuilt, grad_in, grad_spatial, grad_bias.reshape(HID), grad_temporal


def solution(mesh):
    fine = jax.sharding.Mesh(mesh.devices.reshape(2, 8, 2, 2, 4), ("yl", "z", "c", "yh", "x"))
    placed = P(TA, GZ, None, None)
    return jax.shard_map(
        shards,
        mesh=fine,
        in_specs=(placed, placed, P(), P(), P()),
        out_specs=(placed, placed, P(), P(), P()),
        check_vma=False,
    )
```

```python
import math

import jax
import jax.numpy as jnp
from jax import lax
from jax.experimental import pallas as pl
from jax.experimental.pallas import tpu as pltpu
from jax.sharding import PartitionSpec as P

ROWS = 8
COLS = 160
PIX = ROWS * COLS
CH = 32
HID = 64
WIN = 9 * CH
F32 = jnp.float32
BF16 = jnp.bfloat16
VMEM_LIMIT = 24 * 1024 * 1024
EDGES_KIB = 54200
LATE_KIB = 54600
LAST_KIB = 24000
OWN_KIB = 24000
GZ = ("yl", "z", "c")
TA = ("yh", "x")
FLAT = ("yl", "yh", "x", "c")
LONG = pl.CostEstimate(flops=2 * 10**9, bytes_accessed=4 * 10**6, transcendentals=0)
PARAMS = pltpu.CompilerParams(vmem_limit_bytes=VMEM_LIMIT)
IN_VMEM = pl.BlockSpec(memory_space=pltpu.VMEM)
ANYWHERE = pl.BlockSpec(memory_space=pl.ANY)
IN_HBM = pl.BlockSpec(memory_space=pltpu.HBM)


def nn(a, b):
    return lax.dot_general(a, b, (((1,), (0,)), ((), ())), preferred_element_type=F32)


def nt(a, b):
    return lax.dot_general(a, b, (((1,), (1,)), ((), ())), preferred_element_type=F32)


def tn(a, b):
    return lax.dot_general(a, b, (((0,), (0,)), ((), ())), preferred_element_type=F32)


def moved_rows(field, rows):
    if rows == 0:
        return field
    edge = jnp.zeros((field.shape[0], COLS), field.dtype)
    if rows > 0:
        return jnp.concatenate([field[:, COLS:], edge], axis=1)
    return jnp.concatenate([edge, field[:, : PIX - COLS]], axis=1)


def moved_cols(field, cols, col_of):
    if cols == 0:
        return field
    rolled = pltpu.roll(field, (-cols) % PIX, 1)
    return jnp.where(col_of == (COLS - 1 if cols > 0 else 0), jnp.zeros_like(rolled), rolled)


def parities():
    return lax.axis_index("c"), lax.rem(lax.axis_index("x"), 2)


def edges_kernel(fwd_ref, cot_ref, odd_ref, even_ref, far_ref, near_ref, sems):
    core, odd = parities()
    copies = [
        pltpu.make_async_copy(cot_ref.at[pl.ds(odd, 1), :, CH : 2 * CH], odd_ref, sems.at[0]),
        pltpu.make_async_copy(cot_ref.at[pl.ds(1 - odd, 1), :, CH : 2 * CH], even_ref, sems.at[1]),
        pltpu.make_async_copy(fwd_ref.at[:, pl.ds(core, 1), 0:CH], far_ref, sems.at[2]),
        pltpu.make_async_copy(fwd_ref.at[:, pl.ds(1 - core, 1), 0:CH], near_ref, sems.at[3]),
    ]
    for copy in copies:
        copy.start()
    for copy in copies:
        copy.wait()


def weights_kernel(sw_ref, bias_ref, tw_ref, weight_ref, bias_out_ref, tback_ref):
    weight_ref[...] = jnp.concatenate([sw_ref[0], sw_ref[1], sw_ref[2]], axis=1)
    bias_out_ref[...] = jnp.broadcast_to(bias_ref[...], (8, HID)).T[:, 0:1]
    for k in range(3):
        tback_ref[k * CH : (k + 1) * CH] = tw_ref[2 - k]


def hidden_kernel(
    odd_ref, even_ref, far_ref, near_ref, fwd_ref, cot_ref, weight_ref, bias_ref, tback_ref,
    active_ref, hgrad_ref, pay_ref,
    columns, cots,
):
    core, odd = parities()
    col_of = lax.rem(lax.broadcasted_iota(jnp.int32, (CH, PIX), 1), COLS)
    weight = weight_ref[...]
    bias = bias_ref[...]
    tback = tback_ref[...]
    for z in range(2):
        cots[z, 0:32] = jnp.where(odd == 0, odd_ref[0, z], even_ref[0, z])
        cots[z, 32:64] = cot_ref[0, z, CH : 2 * CH]
        cots[z, 64:96] = cot_ref[1, z, CH : 2 * CH]
        cots[z, 96:128] = jnp.where(odd == 0, even_ref[0, z], odd_ref[0, z])
    sgrad = [None, None, None]
    tgrad = None
    bgrad = None

    def unfold(f, p, plane):
        for c in (-1, 0, 1):
            across = moved_cols(plane, c, col_of)
            for r in (-1, 0, 1):
                at = p * WIN + (3 * (r + 1) + c + 1) * CH
                columns[f, at : at + CH, :] = moved_rows(across, r)

    for f in range(2):
        unfold(f, 0, jnp.where(core == 0, far_ref[f, 0], near_ref[f, 0]))
        unfold(f, 1, fwd_ref[f, 0, 0:CH])
        unfold(f, 2, fwd_ref[f, 1, 0:CH])
        unfold(f, 3, jnp.where(core == 0, near_ref[f, 0], far_ref[f, 0]))
        for z in range(2):
            pre = nn(weight, columns[f, z * WIN : (z + 3) * WIN, :]) + bias
            sigma = 1.0 / (1.0 + jnp.exp(-pre))
            active = (pre * sigma).astype(BF16)
            around = cots[z, f * CH : (f + 3) * CH, :]
            through = tn(tback, around)
            hgrad = (through * sigma * (1.0 + pre * (1.0 - sigma))).astype(BF16)
            active_ref[f, z] = active
            hgrad_ref[f, z] = hgrad
            tpart = nt(around, active)
            tgrad = tpart if tgrad is None else tgrad + tpart
            bpart = jnp.sum(hgrad.astype(F32), axis=1, keepdims=True)
            bgrad = bpart if bgrad is None else bgrad + bpart
        both = hgrad_ref[f].reshape(2 * HID, PIX)
        for p in range(4):
            part = nt(both if 0 < p < 3 else hgrad_ref[f, p // 3], columns[f, p * WIN : (p + 1) * WIN, :])
            for z in range(2):
                dz = p - z
                if 0 <= dz < 3:
                    term = part[z * HID : (z + 1) * HID] if 0 < p < 3 else part
                    sgrad[dz] = term if sgrad[dz] is None else sgrad[dz] + term
    for dz in range(3):
        for side in range(2):
            at = (2 * dz + side) * HID
            pay_ref[at : at + HID, :] = sgrad[dz][:, side * 128 : (side + 1) * 128].astype(BF16)
    bhigh, blow = two_parts(bgrad)
    pay_ref[384:448, :] = jnp.concatenate(
        [sgrad[dz][:, 256:288].astype(BF16) for dz in range(3)]
        + [jnp.broadcast_to(bhigh, (HID, 16)), jnp.broadcast_to(blow, (HID, 16))],
        axis=1,
    )
    pay_ref[448:480, :] = jnp.concatenate([tgrad[64:96], tgrad[32:64]], axis=1).astype(BF16)
    pay_ref[480:512, :] = jnp.concatenate([tgrad[0:32], jnp.zeros((32, 64), F32)], axis=1).astype(BF16)


def two_parts(value):
    high = value.astype(BF16)
    return high, (value - high.astype(F32)).astype(BF16)


def sum_kernel(count, got_ref, out_ref):
    rank = ((lax.axis_index("yl") * 2 + lax.axis_index("yh")) * 4 + lax.axis_index("x")) * 2 + lax.axis_index("c")
    total = got_ref[0].astype(F32)
    for i in range(1, got_ref.shape[0]):
        total = total + got_ref[i].astype(F32)
    both = total[:, 96:112] + total[:, 112:128]
    high, low = two_parts(both)
    split = jnp.concatenate([total[:, 0:96].astype(BF16), high, low], axis=1)
    has_bias = jnp.logical_and(rank >= 24, rank < 28)
    out = jnp.where(has_bias, split, total.astype(BF16))
    for i in range(count):
        out_ref[i] = out


def own_kernel(
    act_ref, hg_ref, sw_ref, tw_ref,
    mapped_ref, gin_ref, odd_ref, even_ref, far_ref, near_ref,
):
    core, odd = parities()
    none = jnp.zeros((CH, HID), BF16)
    ahead = jnp.concatenate(
        [
            jnp.concatenate([tw_ref[2], none], axis=1),
            jnp.concatenate([tw_ref[1], tw_ref[2]], axis=1),
            jnp.concatenate([tw_ref[0], tw_ref[1]], axis=1),
            jnp.concatenate([none, tw_ref[0]], axis=1),
        ],
        axis=0,
    )
    for z in range(2):
        mapped = nn(ahead, jnp.concatenate([act_ref[0, z], act_ref[1, z]], axis=0))
        for f in range(2):
            mapped_ref[f, z] = mapped[(f + 1) * CH : (f + 2) * CH]
        sooner, later = mapped[0:CH], mapped[3 * CH : 4 * CH]
        odd_ref[0, z] = jnp.where(odd == 0, sooner, later).astype(BF16)
        even_ref[0, z] = jnp.where(odd == 0, later, sooner).astype(BF16)

    back = jnp.concatenate(
        [
            jnp.concatenate(
                [sw_ref[dz, :, (3 * r + c) * CH : (3 * r + c + 1) * CH] for dz in range(3) for r in range(3)], axis=1
            )
            for c in range(3)
        ],
        axis=0,
    )
    col_of = lax.rem(lax.broadcasted_iota(jnp.int32, (HID, PIX), 1), COLS)

    def rows_joined(lines):
        return lines[CH : 2 * CH] + moved_rows(lines[0:CH], 1) + moved_rows(lines[2 * CH : 3 * CH], -1)

    for f in range(2):
        spread = []
        for z in range(2):
            field = hg_ref[f, z]
            spread.append(tn(back, jnp.concatenate([moved_cols(field, -c, col_of) for c in (-1, 0, 1)], axis=0)))
        below = rows_joined(spread[0][0:96])
        above = rows_joined(spread[1][192:288])
        gin_ref[f, 0] = rows_joined(spread[0][96:192] + spread[1][0:96])
        gin_ref[f, 1] = rows_joined(spread[0][192:288] + spread[1][96:192])
        far_ref[f, 0] = jnp.where(core == 0, below, above).astype(BF16)
        near_ref[f, 0] = jnp.where(core == 0, above, below).astype(BF16)


def rebuilt_kernel(seam_ref, inner_ref, even_ref, mapped_ref, fwd_ref, rebuilt_ref):
    odd = parities()[1]
    place = lax.axis_index("x")
    seam = jnp.logical_or(place == 0, place == lax.axis_size("x") - 1)
    for z in range(2):
        from_odd = jnp.where(seam, seam_ref[0, z], inner_ref[0, z])
        for f in range(2):
            beside = jnp.where(odd == f, from_odd, even_ref[0, z])
            mapped = mapped_ref[f, z] + beside.astype(F32)
            rebuilt_ref[f, z] = (fwd_ref[f, z, CH : 2 * CH].astype(F32) - mapped).astype(BF16)


def gin_kernel(far_ref, near_ref, own_ref, cot_ref, gin_ref):
    core = parities()[0]
    for f in range(2):
        for z in range(2):
            beside = jnp.where(core == z, far_ref[f, 0], near_ref[f, 0])
            back = own_ref[f, z] + beside.astype(F32)
            gin_ref[f, z] = (cot_ref[f, z, 0:CH].astype(F32) + back).astype(BF16)


def grads_kernel(factor, got_ref, gs_ref, gb_ref, gt_ref):
    tail = got_ref[384:448, :].astype(F32) * factor
    for dz in range(3):
        at = 2 * dz * HID
        gs_ref[dz, :, 0:128] = got_ref[at : at + HID, :].astype(F32) * factor
        gs_ref[dz, :, 128:256] = got_ref[at + HID : at + 2 * HID, :].astype(F32) * factor
        gs_ref[dz, :, 256:288] = tail[:, dz * CH : (dz + 1) * CH]
    gb_ref[...] = (tail[:, 96:112] + tail[:, 112:128]).T[0:1]
    taps = got_ref[448:512, :].astype(F32) * factor
    gt_ref[0] = taps[0:32, 0:64]
    gt_ref[1] = taps[0:32, 64:128]
    gt_ref[2] = taps[32:64, 0:64]


def shaped(*dims, dtype=BF16):
    return jax.ShapeDtypeStruct(dims, dtype)


def swaps(pairs):
    return [(a, b) for a, b in pairs] + [(b, a) for a, b in pairs]


def total_of(parts, count, name):
    return pl.pallas_call(
        lambda *refs: sum_kernel(count, *refs),
        in_specs=[IN_VMEM],
        out_specs=IN_VMEM,
        out_shape=shaped(count, 16, 128),
        compiler_params=PARAMS,
        cost_estimate=LONG,
        name=name,
    )(parts)


def finished(kernel, name, operands, kib, cost):
    return pl.pallas_call(
        kernel,
        in_specs=[IN_VMEM] * len(operands),
        out_specs=IN_VMEM,
        out_shape=shaped(2, 2, CH, PIX),
        compiler_params=pltpu.CompilerParams(vmem_limit_bytes=kib * 1024),
        cost_estimate=cost,
        name=name,
    )(*operands)


def shards(outputs_fwd, cotangent, spatial_weight, hidden_bias, temporal_weight):
    gz, ta = lax.axis_size(GZ), lax.axis_size(TA)
    to_far = swaps([(i, i + 1) for i in range(1, gz - 1, 2)])
    to_near = swaps([(i, i + 1) for i in range(0, gz, 2)])
    to_even = swaps([(i, i + 1) for i in range(0, ta, 2)])
    to_odd = swaps([(i, (i + 1) % ta) for i in range(1, ta, 2)])
    row = lax.axis_size("x")
    to_inner = swaps([(i, i + 1) for i in range(1, ta, 2) if (i + 1) % row])
    to_seam = swaps([(i, (i + 1) % ta) for i in range(1, ta, 2) if (i + 1) % row == 0])

    g2_odd, g2_even, y1_far, y1_near = pl.pallas_call(
        edges_kernel,
        in_specs=[IN_HBM] * 2,
        out_specs=[ANYWHERE] * 4,
        out_shape=[shaped(1, 2, CH, PIX)] * 2 + [shaped(2, 1, CH, PIX)] * 2,
        scratch_shapes=[pltpu.SemaphoreType.DMA((4,))],
        compiler_params=pltpu.CompilerParams(vmem_limit_bytes=EDGES_KIB * 1024),
        cost_estimate=pl.CostEstimate(flops=4 * 10**9, bytes_accessed=10**6, transcendentals=0),
        name="edges",
    )(outputs_fwd, cotangent)
    weight, bias, tback = pl.pallas_call(
        weights_kernel,
        in_specs=[IN_VMEM] * 3,
        out_specs=[IN_VMEM] * 3,
        out_shape=[shaped(HID, 3 * WIN), shaped(HID, 1, dtype=F32), shaped(3 * CH, HID)],
        compiler_params=PARAMS,
        name="weights",
    )(spatial_weight, hidden_bias.reshape(1, HID), temporal_weight)
    g2_odd = lax.ppermute(g2_odd, TA, to_odd)
    g2_even = lax.ppermute(g2_even, TA, to_even)
    y1_far = lax.ppermute(y1_far, GZ, to_far)
    y1_near = lax.ppermute(y1_near, GZ, to_near)

    active, hgrad, pay = pl.pallas_call(
        hidden_kernel,
        in_specs=[IN_VMEM] * 9,
        out_specs=[IN_VMEM] * 3,
        out_shape=[shaped(2, 2, HID, PIX)] * 2 + [shaped(512, 128)],
        scratch_shapes=[
            pltpu.VMEM((2, 4 * WIN, PIX), BF16),
            pltpu.VMEM((2, 4 * CH, PIX), BF16),
        ],
        compiler_params=PARAMS,
        cost_estimate=pl.CostEstimate(flops=10**9, bytes_accessed=4 * 10**6, transcendentals=0),
        name="hidden",
    )(g2_odd, g2_even, y1_far, y1_near, outputs_fwd, cotangent, weight, bias, tback)

    parts = lax.all_to_all(pay.reshape(32, 16, 128), FLAT, 0, 0)
    mapped_own, gin_own, map_odd, map_even, gin_far, gin_near = pl.pallas_call(
        own_kernel,
        in_specs=[IN_VMEM] * 4,
        out_specs=[IN_VMEM] * 6,
        out_shape=[shaped(2, 2, CH, PIX, dtype=F32)] * 2
        + [shaped(1, 2, CH, PIX)] * 2
        + [shaped(2, 1, CH, PIX)] * 2,
        compiler_params=pltpu.CompilerParams(vmem_limit_bytes=OWN_KIB * 1024),
        cost_estimate=LONG,
        name="own",
    )(active, hgrad, spatial_weight, temporal_weight)
    map_even = lax.ppermute(map_even, TA, to_even)
    map_inner = lax.ppermute(map_odd, TA, to_inner)
    parts, map_odd = lax.optimization_barrier((parts, map_odd))
    parts = lax.all_to_all(total_of(parts, 8, "plane_sums"), "z", 0, 0)
    map_seam = lax.ppermute(map_odd, TA, to_seam)
    parts, gin_far, gin_near = lax.optimization_barrier((parts, gin_far, gin_near))
    got = lax.all_to_all(total_of(parts, 32, "all_sums"), FLAT, 0, 0)
    rebuilt = finished(
        rebuilt_kernel, "rebuilt", (map_seam, map_inner, map_even, mapped_own, outputs_fwd), LATE_KIB, LONG
    )
    gin_far = lax.ppermute(gin_far, GZ, to_far)
    gin_near = lax.ppermute(gin_near, GZ, to_near)

    got, rebuilt = lax.optimization_barrier((got, rebuilt))

    factor = 1.0 / math.sqrt(2 * ta * 2 * gz * PIX)
    grad_spatial, grad_bias, grad_temporal = pl.pallas_call(
        lambda *refs: grads_kernel(factor, *refs),
        in_specs=[IN_VMEM],
        out_specs=[IN_VMEM] * 3,
        out_shape=[shaped(3, HID, WIN, dtype=F32), shaped(1, HID, dtype=F32), shaped(3, CH, HID, dtype=F32)],
        compiler_params=PARAMS,
        cost_estimate=LONG,
        name="grads",
    )(got.reshape(512, 128))
    gin_own, grad_spatial = lax.optimization_barrier((gin_own, grad_spatial))
    grad_in = finished(gin_kernel, "grad_in", (gin_far, gin_near, gin_own, cotangent), LAST_KIB, LONG)
    return rebuilt, grad_in, grad_spatial, grad_bias.reshape(HID), grad_temporal


def solution(mesh):
    fine = jax.sharding.Mesh(mesh.devices.reshape(2, 8, 2, 2, 4), ("yl", "z", "c", "yh", "x"))
    placed = P(TA, GZ, None, None)
    return jax.shard_map(
        shards,
        mesh=fine,
        in_specs=(placed, placed, P(), P(), P()),
        out_specs=(placed, placed, P(), P(), P()),
        check_vma=False,
    )
```

```python
import math

import jax
import jax.numpy as jnp
from jax import lax
from jax.experimental import pallas as pl
from jax.experimental.pallas import tpu as pltpu
from jax.sharding import PartitionSpec as P

ROWS = 8
COLS = 160
PIX = ROWS * COLS
CH = 32
HID = 64
WIN = 9 * CH
F32 = jnp.float32
BF16 = jnp.bfloat16
VMEM_LIMIT = 24 * 1024 * 1024
EDGES_KIB = 54200
LATE_KIB = 54600
LAST_KIB = 54600
OWN_KIB = 24000
GZ = ("yl", "z", "c")
TA = ("yh", "x")
FLAT = ("yl", "yh", "x", "c")
LONG = pl.CostEstimate(flops=2 * 10**9, bytes_accessed=4 * 10**6, transcendentals=0)
SHORT = pl.CostEstimate(flops=10**6, bytes_accessed=10**5, transcendentals=0)
PARAMS = pltpu.CompilerParams(vmem_limit_bytes=VMEM_LIMIT)
IN_VMEM = pl.BlockSpec(memory_space=pltpu.VMEM)
ANYWHERE = pl.BlockSpec(memory_space=pl.ANY)
IN_HBM = pl.BlockSpec(memory_space=pltpu.HBM)


def nn(a, b):
    return lax.dot_general(a, b, (((1,), (0,)), ((), ())), preferred_element_type=F32)


def nt(a, b):
    return lax.dot_general(a, b, (((1,), (1,)), ((), ())), preferred_element_type=F32)


def tn(a, b):
    return lax.dot_general(a, b, (((0,), (0,)), ((), ())), preferred_element_type=F32)


def moved_rows(field, rows):
    if rows == 0:
        return field
    edge = jnp.zeros((field.shape[0], COLS), field.dtype)
    if rows > 0:
        return jnp.concatenate([field[:, COLS:], edge], axis=1)
    return jnp.concatenate([edge, field[:, : PIX - COLS]], axis=1)


def moved_cols(field, cols, col_of):
    if cols == 0:
        return field
    rolled = pltpu.roll(field, (-cols) % PIX, 1)
    return jnp.where(col_of == (COLS - 1 if cols > 0 else 0), jnp.zeros_like(rolled), rolled)


def parities():
    return lax.axis_index("c"), lax.rem(lax.axis_index("x"), 2)


def edges_kernel(fwd_ref, cot_ref, odd_ref, even_ref, far_ref, near_ref, sems):
    core, odd = parities()
    copies = [
        pltpu.make_async_copy(cot_ref.at[pl.ds(odd, 1), :, CH : 2 * CH], odd_ref, sems.at[0]),
        pltpu.make_async_copy(cot_ref.at[pl.ds(1 - odd, 1), :, CH : 2 * CH], even_ref, sems.at[1]),
        pltpu.make_async_copy(fwd_ref.at[:, pl.ds(core, 1), 0:CH], far_ref, sems.at[2]),
        pltpu.make_async_copy(fwd_ref.at[:, pl.ds(1 - core, 1), 0:CH], near_ref, sems.at[3]),
    ]
    for copy in copies:
        copy.start()
    for copy in copies:
        copy.wait()


def weights_kernel(sw_ref, bias_ref, tw_ref, weight_ref, bias_out_ref, tback_ref):
    weight_ref[...] = jnp.concatenate([sw_ref[0], sw_ref[1], sw_ref[2]], axis=1)
    bias_out_ref[...] = jnp.broadcast_to(bias_ref[...], (8, HID)).T[:, 0:1]
    for k in range(3):
        tback_ref[k * CH : (k + 1) * CH] = tw_ref[2 - k]


def hidden_kernel(
    odd_ref, even_ref, far_ref, near_ref, fwd_ref, cot_ref, weight_ref, bias_ref, tback_ref,
    active_ref, hgrad_ref, pay_ref,
    columns, cots,
):
    core, odd = parities()
    col_of = lax.rem(lax.broadcasted_iota(jnp.int32, (CH, PIX), 1), COLS)
    weight = weight_ref[...]
    bias = bias_ref[...]
    tback = tback_ref[...]
    for z in range(2):
        cots[z, 0:32] = jnp.where(odd == 0, odd_ref[0, z], even_ref[0, z])
        cots[z, 32:64] = cot_ref[0, z, CH : 2 * CH]
        cots[z, 64:96] = cot_ref[1, z, CH : 2 * CH]
        cots[z, 96:128] = jnp.where(odd == 0, even_ref[0, z], odd_ref[0, z])
    sgrad = [None, None, None]
    tgrad = None
    bgrad = None

    def unfold(f, p, plane):
        for c in (-1, 0, 1):
            across = moved_cols(plane, c, col_of)
            for r in (-1, 0, 1):
                at = p * WIN + (3 * (r + 1) + c + 1) * CH
                columns[f, at : at + CH, :] = moved_rows(across, r)

    for f in range(2):
        unfold(f, 0, jnp.where(core == 0, far_ref[f, 0], near_ref[f, 0]))
        unfold(f, 1, fwd_ref[f, 0, 0:CH])
        unfold(f, 2, fwd_ref[f, 1, 0:CH])
        unfold(f, 3, jnp.where(core == 0, near_ref[f, 0], far_ref[f, 0]))
        for z in range(2):
            pre = nn(weight, columns[f, z * WIN : (z + 3) * WIN, :]) + bias
            sigma = 1.0 / (1.0 + jnp.exp(-pre))
            active = (pre * sigma).astype(BF16)
            around = cots[z, f * CH : (f + 3) * CH, :]
            through = tn(tback, around)
            hgrad = (through * sigma * (1.0 + pre * (1.0 - sigma))).astype(BF16)
            active_ref[f, z] = active
            hgrad_ref[f, z] = hgrad
            tpart = nt(around, active)
            tgrad = tpart if tgrad is None else tgrad + tpart
            bpart = jnp.sum(hgrad.astype(F32), axis=1, keepdims=True)
            bgrad = bpart if bgrad is None else bgrad + bpart
        both = hgrad_ref[f].reshape(2 * HID, PIX)
        for p in range(4):
            part = nt(both if 0 < p < 3 else hgrad_ref[f, p // 3], columns[f, p * WIN : (p + 1) * WIN, :])
            for z in range(2):
                dz = p - z
                if 0 <= dz < 3:
                    term = part[z * HID : (z + 1) * HID] if 0 < p < 3 else part
                    sgrad[dz] = term if sgrad[dz] is None else sgrad[dz] + term
    for dz in range(3):
        for side in range(2):
            at = (2 * dz + side) * HID
            pay_ref[at : at + HID, :] = sgrad[dz][:, side * 128 : (side + 1) * 128].astype(BF16)
    bhigh, blow = two_parts(bgrad)
    pay_ref[384:448, :] = jnp.concatenate(
        [sgrad[dz][:, 256:288].astype(BF16) for dz in range(3)]
        + [jnp.broadcast_to(bhigh, (HID, 16)), jnp.broadcast_to(blow, (HID, 16))],
        axis=1,
    )
    pay_ref[448:480, :] = jnp.concatenate([tgrad[64:96], tgrad[32:64]], axis=1).astype(BF16)
    pay_ref[480:512, :] = jnp.concatenate([tgrad[0:32], jnp.zeros((32, 64), F32)], axis=1).astype(BF16)


def two_parts(value):
    high = value.astype(BF16)
    return high, (value - high.astype(F32)).astype(BF16)


def sum_kernel(count, got_ref, out_ref):
    rank = ((lax.axis_index("yl") * 2 + lax.axis_index("yh")) * 4 + lax.axis_index("x")) * 2 + lax.axis_index("c")
    total = got_ref[0].astype(F32)
    for i in range(1, got_ref.shape[0]):
        total = total + got_ref[i].astype(F32)
    both = total[:, 96:112] + total[:, 112:128]
    high, low = two_parts(both)
    split = jnp.concatenate([total[:, 0:96].astype(BF16), high, low], axis=1)
    has_bias = jnp.logical_and(rank >= 24, rank < 28)
    out = jnp.where(has_bias, split, total.astype(BF16))
    for i in range(count):
        out_ref[i] = out


def own_kernel(
    act_ref, hg_ref, sw_ref, tw_ref,
    mapped_ref, gin_ref, odd_ref, even_ref, far_ref, near_ref,
):
    core, odd = parities()
    none = jnp.zeros((CH, HID), BF16)
    ahead = jnp.concatenate(
        [
            jnp.concatenate([tw_ref[2], none], axis=1),
            jnp.concatenate([tw_ref[1], tw_ref[2]], axis=1),
            jnp.concatenate([tw_ref[0], tw_ref[1]], axis=1),
            jnp.concatenate([none, tw_ref[0]], axis=1),
        ],
        axis=0,
    )
    for z in range(2):
        mapped = nn(ahead, jnp.concatenate([act_ref[0, z], act_ref[1, z]], axis=0))
        for f in range(2):
            mapped_ref[f, z] = mapped[(f + 1) * CH : (f + 2) * CH]
        sooner, later = mapped[0:CH], mapped[3 * CH : 4 * CH]
        odd_ref[0, z] = jnp.where(odd == 0, sooner, later).astype(BF16)
        even_ref[0, z] = jnp.where(odd == 0, later, sooner).astype(BF16)

    back = jnp.concatenate(
        [
            jnp.concatenate(
                [sw_ref[dz, :, (3 * r + c) * CH : (3 * r + c + 1) * CH] for dz in range(3) for r in range(3)], axis=1
            )
            for c in range(3)
        ],
        axis=0,
    )
    col_of = lax.rem(lax.broadcasted_iota(jnp.int32, (HID, PIX), 1), COLS)

    def rows_joined(lines):
        return lines[CH : 2 * CH] + moved_rows(lines[0:CH], 1) + moved_rows(lines[2 * CH : 3 * CH], -1)

    for f in range(2):
        spread = []
        for z in range(2):
            field = hg_ref[f, z]
            spread.append(tn(back, jnp.concatenate([moved_cols(field, -c, col_of) for c in (-1, 0, 1)], axis=0)))
        below = rows_joined(spread[0][0:96])
        above = rows_joined(spread[1][192:288])
        gin_ref[f, 0] = rows_joined(spread[0][96:192] + spread[1][0:96])
        gin_ref[f, 1] = rows_joined(spread[0][192:288] + spread[1][96:192])
        far_ref[f, 0] = jnp.where(core == 0, below, above).astype(BF16)
        near_ref[f, 0] = jnp.where(core == 0, above, below).astype(BF16)


def rebuilt_kernel(seam_ref, inner_ref, even_ref, mapped_ref, fwd_ref, rebuilt_ref):
    odd = parities()[1]
    place = lax.axis_index("x")
    seam = jnp.logical_or(place == 0, place == lax.axis_size("x") - 1)
    for z in range(2):
        from_odd = jnp.where(seam, seam_ref[0, z], inner_ref[0, z])
        for f in range(2):
            beside = jnp.where(odd == f, from_odd, even_ref[0, z])
            mapped = mapped_ref[f, z] + beside.astype(F32)
            rebuilt_ref[f, z] = (fwd_ref[f, z, CH : 2 * CH].astype(F32) - mapped).astype(BF16)


def gin_kernel(far_ref, near_ref, own_ref, cot_ref, gin_ref):
    core = parities()[0]
    for f in range(2):
        for z in range(2):
            beside = jnp.where(core == z, far_ref[f, 0], near_ref[f, 0])
            back = own_ref[f, z] + beside.astype(F32)
            gin_ref[f, z] = (cot_ref[f, z, 0:CH].astype(F32) + back).astype(BF16)


def grads_kernel(factor, got_ref, gs_ref, gb_ref, gt_ref):
    tail = got_ref[384:448, :].astype(F32) * factor
    for dz in range(3):
        at = 2 * dz * HID
        gs_ref[dz, :, 0:128] = got_ref[at : at + HID, :].astype(F32) * factor
        gs_ref[dz, :, 128:256] = got_ref[at + HID : at + 2 * HID, :].astype(F32) * factor
        gs_ref[dz, :, 256:288] = tail[:, dz * CH : (dz + 1) * CH]
    gb_ref[...] = (tail[:, 96:112] + tail[:, 112:128]).T[0:1]
    taps = got_ref[448:512, :].astype(F32) * factor
    gt_ref[0] = taps[0:32, 0:64]
    gt_ref[1] = taps[0:32, 64:128]
    gt_ref[2] = taps[32:64, 0:64]


def shaped(*dims, dtype=BF16):
    return jax.ShapeDtypeStruct(dims, dtype)


def swaps(pairs):
    return [(a, b) for a, b in pairs] + [(b, a) for a, b in pairs]


def total_of(parts, count, name):
    return pl.pallas_call(
        lambda *refs: sum_kernel(count, *refs),
        in_specs=[IN_VMEM],
        out_specs=IN_VMEM,
        out_shape=shaped(count, 16, 128),
        compiler_params=PARAMS,
        cost_estimate=LONG,
        name=name,
    )(parts)


def finished(kernel, name, operands, kib, cost):
    return pl.pallas_call(
        kernel,
        in_specs=[IN_VMEM] * len(operands),
        out_specs=IN_VMEM,
        out_shape=shaped(2, 2, CH, PIX),
        compiler_params=pltpu.CompilerParams(vmem_limit_bytes=kib * 1024),
        cost_estimate=cost,
        name=name,
    )(*operands)


def shards(outputs_fwd, cotangent, spatial_weight, hidden_bias, temporal_weight):
    gz, ta = lax.axis_size(GZ), lax.axis_size(TA)
    to_far = swaps([(i, i + 1) for i in range(1, gz - 1, 2)])
    to_near = swaps([(i, i + 1) for i in range(0, gz, 2)])
    to_even = swaps([(i, i + 1) for i in range(0, ta, 2)])
    to_odd = swaps([(i, (i + 1) % ta) for i in range(1, ta, 2)])
    row = lax.axis_size("x")
    to_inner = swaps([(i, i + 1) for i in range(1, ta, 2) if (i + 1) % row])
    to_seam = swaps([(i, (i + 1) % ta) for i in range(1, ta, 2) if (i + 1) % row == 0])

    g2_odd, g2_even, y1_far, y1_near = pl.pallas_call(
        edges_kernel,
        in_specs=[IN_HBM] * 2,
        out_specs=[ANYWHERE] * 4,
        out_shape=[shaped(1, 2, CH, PIX)] * 2 + [shaped(2, 1, CH, PIX)] * 2,
        scratch_shapes=[pltpu.SemaphoreType.DMA((4,))],
        compiler_params=pltpu.CompilerParams(vmem_limit_bytes=EDGES_KIB * 1024),
        cost_estimate=pl.CostEstimate(flops=4 * 10**9, bytes_accessed=10**6, transcendentals=0),
        name="edges",
    )(outputs_fwd, cotangent)
    weight, bias, tback = pl.pallas_call(
        weights_kernel,
        in_specs=[IN_VMEM] * 3,
        out_specs=[IN_VMEM] * 3,
        out_shape=[shaped(HID, 3 * WIN), shaped(HID, 1, dtype=F32), shaped(3 * CH, HID)],
        compiler_params=PARAMS,
        name="weights",
    )(spatial_weight, hidden_bias.reshape(1, HID), temporal_weight)
    g2_odd = lax.ppermute(g2_odd, TA, to_odd)
    g2_even = lax.ppermute(g2_even, TA, to_even)
    y1_far = lax.ppermute(y1_far, GZ, to_far)
    y1_near = lax.ppermute(y1_near, GZ, to_near)

    active, hgrad, pay = pl.pallas_call(
        hidden_kernel,
        in_specs=[IN_VMEM] * 9,
        out_specs=[IN_VMEM] * 3,
        out_shape=[shaped(2, 2, HID, PIX)] * 2 + [shaped(512, 128)],
        scratch_shapes=[
            pltpu.VMEM((2, 4 * WIN, PIX), BF16),
            pltpu.VMEM((2, 4 * CH, PIX), BF16),
        ],
        compiler_params=PARAMS,
        cost_estimate=pl.CostEstimate(flops=10**9, bytes_accessed=4 * 10**6, transcendentals=0),
        name="hidden",
    )(g2_odd, g2_even, y1_far, y1_near, outputs_fwd, cotangent, weight, bias, tback)

    parts = lax.all_to_all(pay.reshape(32, 16, 128), FLAT, 0, 0)
    mapped_own, gin_own, map_odd, map_even, gin_far, gin_near = pl.pallas_call(
        own_kernel,
        in_specs=[IN_VMEM] * 4,
        out_specs=[IN_VMEM] * 6,
        out_shape=[shaped(2, 2, CH, PIX, dtype=F32)] * 2
        + [shaped(1, 2, CH, PIX)] * 2
        + [shaped(2, 1, CH, PIX)] * 2,
        compiler_params=pltpu.CompilerParams(vmem_limit_bytes=OWN_KIB * 1024),
        cost_estimate=LONG,
        name="own",
    )(active, hgrad, spatial_weight, temporal_weight)
    gin_far = lax.ppermute(gin_far, GZ, to_far)
    gin_near = lax.ppermute(gin_near, GZ, to_near)
    parts, map_odd, map_even = lax.optimization_barrier((parts, map_odd, map_even))
    parts = lax.all_to_all(total_of(parts, 8, "plane_sums"), "z", 0, 0)
    map_even = lax.ppermute(map_even, TA, to_even)
    map_inner = lax.ppermute(map_odd, TA, to_inner)
    map_seam = lax.ppermute(map_odd, TA, to_seam)
    parts, gin_far, gin_near = lax.optimization_barrier((parts, gin_far, gin_near))
    got = lax.all_to_all(total_of(parts, 32, "all_sums"), FLAT, 0, 0)
    rebuilt = finished(
        rebuilt_kernel, "rebuilt", (map_seam, map_inner, map_even, mapped_own, outputs_fwd), LATE_KIB, LONG
    )
    grad_in = finished(gin_kernel, "grad_in", (gin_far, gin_near, gin_own, cotangent), LAST_KIB, SHORT)
    got, rebuilt, grad_in = lax.optimization_barrier((got, rebuilt, grad_in))

    factor = 1.0 / math.sqrt(2 * ta * 2 * gz * PIX)
    grad_spatial, grad_bias, grad_temporal = pl.pallas_call(
        lambda *refs: grads_kernel(factor, *refs),
        in_specs=[IN_VMEM],
        out_specs=[IN_VMEM] * 3,
        out_shape=[shaped(3, HID, WIN, dtype=F32), shaped(1, HID, dtype=F32), shaped(3, CH, HID, dtype=F32)],
        compiler_params=PARAMS,
        cost_estimate=LONG,
        name="grads",
    )(got.reshape(512, 128))
    return rebuilt, grad_in, grad_spatial, grad_bias.reshape(HID), grad_temporal


def solution(mesh):
    fine = jax.sharding.Mesh(mesh.devices.reshape(2, 8, 2, 2, 4), ("yl", "z", "c", "yh", "x"))
    placed = P(TA, GZ, None, None)
    return jax.shard_map(
        shards,
        mesh=fine,
        in_specs=(placed, placed, P(), P(), P()),
        out_specs=(placed, placed, P(), P(), P()),
        check_vma=False,
    )
```

```python
import math

import jax
import jax.numpy as jnp
from jax import lax
from jax.experimental import pallas as pl
from jax.experimental.pallas import tpu as pltpu
from jax.sharding import PartitionSpec as P

ROWS = 8
COLS = 160
PIX = ROWS * COLS
CH = 32
HID = 64
WIN = 9 * CH
F32 = jnp.float32
BF16 = jnp.bfloat16
VMEM_LIMIT = 24 * 1024 * 1024
EDGES_KIB = 54200
LATE_KIB = 54600
LAST_KIB = 54600
OWN_KIB = 24000
GZ = ("yl", "z", "c")
TA = ("yh", "x")
FLAT = ("yl", "yh", "x", "c")
LONG = pl.CostEstimate(flops=2 * 10**9, bytes_accessed=4 * 10**6, transcendentals=0)
SHORT = pl.CostEstimate(flops=10**6, bytes_accessed=10**5, transcendentals=0)
PARAMS = pltpu.CompilerParams(vmem_limit_bytes=VMEM_LIMIT)
IN_VMEM = pl.BlockSpec(memory_space=pltpu.VMEM)
ANYWHERE = pl.BlockSpec(memory_space=pl.ANY)
IN_HBM = pl.BlockSpec(memory_space=pltpu.HBM)


def nn(a, b):
    return lax.dot_general(a, b, (((1,), (0,)), ((), ())), preferred_element_type=F32)


def nt(a, b):
    return lax.dot_general(a, b, (((1,), (1,)), ((), ())), preferred_element_type=F32)


def tn(a, b):
    return lax.dot_general(a, b, (((0,), (0,)), ((), ())), preferred_element_type=F32)


def moved_rows(field, rows):
    if rows == 0:
        return field
    edge = jnp.zeros((field.shape[0], COLS), field.dtype)
    if rows > 0:
        return jnp.concatenate([field[:, COLS:], edge], axis=1)
    return jnp.concatenate([edge, field[:, : PIX - COLS]], axis=1)


def moved_cols(field, cols, col_of):
    if cols == 0:
        return field
    rolled = pltpu.roll(field, (-cols) % PIX, 1)
    return jnp.where(col_of == (COLS - 1 if cols > 0 else 0), jnp.zeros_like(rolled), rolled)


def parities():
    return lax.axis_index("c"), lax.rem(lax.axis_index("x"), 2)


def edges_kernel(fwd_ref, cot_ref, odd_ref, even_ref, far_ref, near_ref, sems):
    core, odd = parities()
    copies = [
        pltpu.make_async_copy(cot_ref.at[pl.ds(odd, 1), :, CH : 2 * CH], odd_ref, sems.at[0]),
        pltpu.make_async_copy(cot_ref.at[pl.ds(1 - odd, 1), :, CH : 2 * CH], even_ref, sems.at[1]),
        pltpu.make_async_copy(fwd_ref.at[:, pl.ds(core, 1), 0:CH], far_ref, sems.at[2]),
        pltpu.make_async_copy(fwd_ref.at[:, pl.ds(1 - core, 1), 0:CH], near_ref, sems.at[3]),
    ]
    for copy in copies:
        copy.start()
    for copy in copies:
        copy.wait()


def weights_kernel(sw_ref, bias_ref, tw_ref, weight_ref, bias_out_ref, tback_ref):
    weight_ref[...] = jnp.concatenate([sw_ref[0], sw_ref[1], sw_ref[2]], axis=1)
    bias_out_ref[...] = jnp.broadcast_to(bias_ref[...], (8, HID)).T[:, 0:1]
    for k in range(3):
        tback_ref[k * CH : (k + 1) * CH] = tw_ref[2 - k]


def hidden_kernel(
    odd_ref, even_ref, far_ref, near_ref, fwd_ref, cot_ref, weight_ref, bias_ref, tback_ref,
    active_ref, hgrad_ref, pay_ref,
    columns, cots,
):
    core, odd = parities()
    col_of = lax.rem(lax.broadcasted_iota(jnp.int32, (CH, PIX), 1), COLS)
    weight = weight_ref[...]
    bias = bias_ref[...]
    tback = tback_ref[...]
    for z in range(2):
        cots[z, 0:32] = jnp.where(odd == 0, odd_ref[0, z], even_ref[0, z])
        cots[z, 32:64] = cot_ref[0, z, CH : 2 * CH]
        cots[z, 64:96] = cot_ref[1, z, CH : 2 * CH]
        cots[z, 96:128] = jnp.where(odd == 0, even_ref[0, z], odd_ref[0, z])
    sgrad = [None, None, None]
    tgrad = None
    bgrad = None

    def unfold(f, p, plane):
        for c in (-1, 0, 1):
            across = moved_cols(plane, c, col_of)
            for r in (-1, 0, 1):
                at = p * WIN + (3 * (r + 1) + c + 1) * CH
                columns[f, at : at + CH, :] = moved_rows(across, r)

    for f in range(2):
        unfold(f, 0, jnp.where(core == 0, far_ref[f, 0], near_ref[f, 0]))
        unfold(f, 1, fwd_ref[f, 0, 0:CH])
        unfold(f, 2, fwd_ref[f, 1, 0:CH])
        unfold(f, 3, jnp.where(core == 0, near_ref[f, 0], far_ref[f, 0]))
        for z in range(2):
            pre = nn(weight, columns[f, z * WIN : (z + 3) * WIN, :]) + bias
            sigma = 1.0 / (1.0 + jnp.exp(-pre))
            active = (pre * sigma).astype(BF16)
            around = cots[z, f * CH : (f + 3) * CH, :]
            through = tn(tback, around)
            hgrad = (through * sigma * (1.0 + pre * (1.0 - sigma))).astype(BF16)
            active_ref[f, z] = active
            hgrad_ref[f, z] = hgrad
            tpart = nt(around, active)
            tgrad = tpart if tgrad is None else tgrad + tpart
            bpart = jnp.sum(hgrad.astype(F32), axis=1, keepdims=True)
            bgrad = bpart if bgrad is None else bgrad + bpart
        both = hgrad_ref[f].reshape(2 * HID, PIX)
        for p in range(4):
            part = nt(both if 0 < p < 3 else hgrad_ref[f, p // 3], columns[f, p * WIN : (p + 1) * WIN, :])
            for z in range(2):
                dz = p - z
                if 0 <= dz < 3:
                    term = part[z * HID : (z + 1) * HID] if 0 < p < 3 else part
                    sgrad[dz] = term if sgrad[dz] is None else sgrad[dz] + term
    for dz in range(3):
        for side in range(2):
            at = (2 * dz + side) * HID
            pay_ref[at : at + HID, :] = sgrad[dz][:, side * 128 : (side + 1) * 128].astype(BF16)
    bhigh, blow = two_parts(bgrad)
    pay_ref[384:448, :] = jnp.concatenate(
        [sgrad[dz][:, 256:288].astype(BF16) for dz in range(3)]
        + [jnp.broadcast_to(bhigh, (HID, 16)), jnp.broadcast_to(blow, (HID, 16))],
        axis=1,
    )
    pay_ref[448:480, :] = jnp.concatenate([tgrad[64:96], tgrad[32:64]], axis=1).astype(BF16)
    pay_ref[480:512, :] = jnp.concatenate([tgrad[0:32], jnp.zeros((32, 64), F32)], axis=1).astype(BF16)


def two_parts(value):
    high = value.astype(BF16)
    return high, (value - high.astype(F32)).astype(BF16)


def sum_kernel(count, got_ref, out_ref):
    rank = ((lax.axis_index("yl") * 2 + lax.axis_index("yh")) * 4 + lax.axis_index("x")) * 2 + lax.axis_index("c")
    total = got_ref[0].astype(F32)
    for i in range(1, got_ref.shape[0]):
        total = total + got_ref[i].astype(F32)
    both = total[:, 96:112] + total[:, 112:128]
    high, low = two_parts(both)
    split = jnp.concatenate([total[:, 0:96].astype(BF16), high, low], axis=1)
    has_bias = jnp.logical_and(rank >= 24, rank < 28)
    out = jnp.where(has_bias, split, total.astype(BF16))
    for i in range(count):
        out_ref[i] = out


def own_kernel(
    act_ref, hg_ref, sw_ref, tw_ref,
    mapped_ref, gin_ref, odd_ref, even_ref, far_ref, near_ref,
):
    core, odd = parities()
    none = jnp.zeros((CH, HID), BF16)
    ahead = jnp.concatenate(
        [
            jnp.concatenate([tw_ref[2], none], axis=1),
            jnp.concatenate([tw_ref[1], tw_ref[2]], axis=1),
            jnp.concatenate([tw_ref[0], tw_ref[1]], axis=1),
            jnp.concatenate([none, tw_ref[0]], axis=1),
        ],
        axis=0,
    )
    for z in range(2):
        mapped = nn(ahead, jnp.concatenate([act_ref[0, z], act_ref[1, z]], axis=0))
        for f in range(2):
            mapped_ref[f, z] = mapped[(f + 1) * CH : (f + 2) * CH]
        sooner, later = mapped[0:CH], mapped[3 * CH : 4 * CH]
        odd_ref[0, z] = jnp.where(odd == 0, sooner, later).astype(BF16)
        even_ref[0, z] = jnp.where(odd == 0, later, sooner).astype(BF16)

    back = jnp.concatenate(
        [
            jnp.concatenate(
                [sw_ref[dz, :, (3 * r + c) * CH : (3 * r + c + 1) * CH] for dz in range(3) for r in range(3)], axis=1
            )
            for c in range(3)
        ],
        axis=0,
    )
    col_of = lax.rem(lax.broadcasted_iota(jnp.int32, (HID, PIX), 1), COLS)

    def rows_joined(lines):
        return lines[CH : 2 * CH] + moved_rows(lines[0:CH], 1) + moved_rows(lines[2 * CH : 3 * CH], -1)

    for f in range(2):
        spread = []
        for z in range(2):
            field = hg_ref[f, z]
            spread.append(tn(back, jnp.concatenate([moved_cols(field, -c, col_of) for c in (-1, 0, 1)], axis=0)))
        below = rows_joined(spread[0][0:96])
        above = rows_joined(spread[1][192:288])
        gin_ref[f, 0] = rows_joined(spread[0][96:192] + spread[1][0:96])
        gin_ref[f, 1] = rows_joined(spread[0][192:288] + spread[1][96:192])
        far_ref[f, 0] = jnp.where(core == 0, below, above).astype(BF16)
        near_ref[f, 0] = jnp.where(core == 0, above, below).astype(BF16)


def rebuilt_kernel(odd_ref, even_ref, mapped_ref, fwd_ref, rebuilt_ref):
    odd = parities()[1]
    for z in range(2):
        for f in range(2):
            beside = jnp.where(odd == f, odd_ref[0, z], even_ref[0, z])
            mapped = mapped_ref[f, z] + beside.astype(F32)
            rebuilt_ref[f, z] = (fwd_ref[f, z, CH : 2 * CH].astype(F32) - mapped).astype(BF16)


def gin_kernel(far_ref, near_ref, own_ref, cot_ref, gin_ref):
    core = parities()[0]
    for f in range(2):
        for z in range(2):
            beside = jnp.where(core == z, far_ref[f, 0], near_ref[f, 0])
            back = own_ref[f, z] + beside.astype(F32)
            gin_ref[f, z] = (cot_ref[f, z, 0:CH].astype(F32) + back).astype(BF16)


def grads_kernel(factor, got_ref, gs_ref, gb_ref, gt_ref):
    tail = got_ref[384:448, :].astype(F32) * factor
    for dz in range(3):
        at = 2 * dz * HID
        gs_ref[dz, :, 0:128] = got_ref[at : at + HID, :].astype(F32) * factor
        gs_ref[dz, :, 128:256] = got_ref[at + HID : at + 2 * HID, :].astype(F32) * factor
        gs_ref[dz, :, 256:288] = tail[:, dz * CH : (dz + 1) * CH]
    gb_ref[...] = (tail[:, 96:112] + tail[:, 112:128]).T[0:1]
    taps = got_ref[448:512, :].astype(F32) * factor
    gt_ref[0] = taps[0:32, 0:64]
    gt_ref[1] = taps[0:32, 64:128]
    gt_ref[2] = taps[32:64, 0:64]


def shaped(*dims, dtype=BF16):
    return jax.ShapeDtypeStruct(dims, dtype)


def swaps(pairs):
    return [(a, b) for a, b in pairs] + [(b, a) for a, b in pairs]


def total_of(parts, count, name):
    return pl.pallas_call(
        lambda *refs: sum_kernel(count, *refs),
        in_specs=[IN_VMEM],
        out_specs=IN_VMEM,
        out_shape=shaped(count, 16, 128),
        compiler_params=PARAMS,
        cost_estimate=LONG,
        name=name,
    )(parts)


def finished(kernel, name, operands, kib, cost):
    return pl.pallas_call(
        kernel,
        in_specs=[IN_VMEM] * len(operands),
        out_specs=IN_VMEM,
        out_shape=shaped(2, 2, CH, PIX),
        compiler_params=pltpu.CompilerParams(vmem_limit_bytes=kib * 1024),
        cost_estimate=cost,
        name=name,
    )(*operands)


def shards(outputs_fwd, cotangent, spatial_weight, hidden_bias, temporal_weight):
    gz, ta = lax.axis_size(GZ), lax.axis_size(TA)
    to_far = swaps([(i, i + 1) for i in range(1, gz - 1, 2)])
    to_near = swaps([(i, i + 1) for i in range(0, gz, 2)])
    to_even = swaps([(i, i + 1) for i in range(0, ta, 2)])
    to_odd = swaps([(i, (i + 1) % ta) for i in range(1, ta, 2)])

    g2_odd, g2_even, y1_far, y1_near = pl.pallas_call(
        edges_kernel,
        in_specs=[IN_HBM] * 2,
        out_specs=[ANYWHERE] * 4,
        out_shape=[shaped(1, 2, CH, PIX)] * 2 + [shaped(2, 1, CH, PIX)] * 2,
        scratch_shapes=[pltpu.SemaphoreType.DMA((4,))],
        compiler_params=pltpu.CompilerParams(vmem_limit_bytes=EDGES_KIB * 1024),
        cost_estimate=pl.CostEstimate(flops=4 * 10**9, bytes_accessed=10**6, transcendentals=0),
        name="edges",
    )(outputs_fwd, cotangent)
    weight, bias, tback = pl.pallas_call(
        weights_kernel,
        in_specs=[IN_VMEM] * 3,
        out_specs=[IN_VMEM] * 3,
        out_shape=[shaped(HID, 3 * WIN), shaped(HID, 1, dtype=F32), shaped(3 * CH, HID)],
        compiler_params=PARAMS,
        name="weights",
    )(spatial_weight, hidden_bias.reshape(1, HID), temporal_weight)
    g2_odd = lax.ppermute(g2_odd, TA, to_odd)
    g2_even = lax.ppermute(g2_even, TA, to_even)
    y1_far = lax.ppermute(y1_far, GZ, to_far)
    y1_near = lax.ppermute(y1_near, GZ, to_near)

    active, hgrad, pay = pl.pallas_call(
        hidden_kernel,
        in_specs=[IN_VMEM] * 9,
        out_specs=[IN_VMEM] * 3,
        out_shape=[shaped(2, 2, HID, PIX)] * 2 + [shaped(512, 128)],
        scratch_shapes=[
            pltpu.VMEM((2, 4 * WIN, PIX), BF16),
            pltpu.VMEM((2, 4 * CH, PIX), BF16),
        ],
        compiler_params=PARAMS,
        cost_estimate=pl.CostEstimate(flops=10**9, bytes_accessed=4 * 10**6, transcendentals=0),
        name="hidden",
    )(g2_odd, g2_even, y1_far, y1_near, outputs_fwd, cotangent, weight, bias, tback)

    parts = lax.all_to_all(pay.reshape(32, 16, 128), FLAT, 0, 0)
    mapped_own, gin_own, map_odd, map_even, gin_far, gin_near = pl.pallas_call(
        own_kernel,
        in_specs=[IN_VMEM] * 4,
        out_specs=[IN_VMEM] * 6,
        out_shape=[shaped(2, 2, CH, PIX, dtype=F32)] * 2
        + [shaped(1, 2, CH, PIX)] * 2
        + [shaped(2, 1, CH, PIX)] * 2,
        compiler_params=pltpu.CompilerParams(vmem_limit_bytes=OWN_KIB * 1024),
        cost_estimate=LONG,
        name="own",
    )(active, hgrad, spatial_weight, temporal_weight)
    gin_far = lax.ppermute(gin_far, GZ, to_far)
    gin_near = lax.ppermute(gin_near, GZ, to_near)
    parts, map_odd, map_even = lax.optimization_barrier((parts, map_odd, map_even))
    parts = lax.all_to_all(total_of(parts, 8, "plane_sums"), "z", 0, 0)
    map_odd = lax.ppermute(map_odd, TA, to_odd)
    map_even = lax.ppermute(map_even, TA, to_even)
    parts, gin_far, gin_near = lax.optimization_barrier((parts, gin_far, gin_near))
    got = lax.all_to_all(total_of(parts, 32, "all_sums"), FLAT, 0, 0)
    rebuilt = finished(
        rebuilt_kernel, "rebuilt", (map_odd, map_even, mapped_own, outputs_fwd), LATE_KIB, LONG
    )
    grad_in = finished(gin_kernel, "grad_in", (gin_far, gin_near, gin_own, cotangent), LAST_KIB, SHORT)
    got, rebuilt, grad_in = lax.optimization_barrier((got, rebuilt, grad_in))

    factor = 1.0 / math.sqrt(2 * ta * 2 * gz * PIX)
    grad_spatial, grad_bias, grad_temporal = pl.pallas_call(
        lambda *refs: grads_kernel(factor, *refs),
        in_specs=[IN_VMEM],
        out_specs=[IN_VMEM] * 3,
        out_shape=[shaped(3, HID, WIN, dtype=F32), shaped(1, HID, dtype=F32), shaped(3, CH, HID, dtype=F32)],
        compiler_params=PARAMS,
        cost_estimate=LONG,
        name="grads",
    )(got.reshape(512, 128))
    return rebuilt, grad_in, grad_spatial, grad_bias.reshape(HID), grad_temporal


def solution(mesh):
    fine = jax.sharding.Mesh(mesh.devices.reshape(2, 8, 2, 2, 4), ("yl", "z", "c", "yh", "x"))
    placed = P(TA, GZ, None, None)
    return jax.shard_map(
        shards,
        mesh=fine,
        in_specs=(placed, placed, P(), P(), P()),
        out_specs=(placed, placed, P(), P(), P()),
        check_vma=False,
    )
```
